256 devices in a mesh: seq: 32 (over x, y, core), tp: 8 (over z).
Axes of the slice: x: 4, y: 4, z: 8, core: 2. Of those that a mesh axis runs over, the one named last changes fastest.
Arguments:
- hidden: bfloat16 [40960, 8192], P('seq', 'tp'), may hold values from -6 to 6
- queries: bfloat16 [40960, 8192], P('seq', 'tp'), may hold values from -8 to 8
- keys_values: bfloat16 [2, 40960, 1024], P(None, 'seq', 'tp'), may hold values from -8 to 8
- w_router: bfloat16 [8192], P('tp'), may hold values from -0.0625 to 0.0625
- routed: int32 [32, 160], P('seq'), may hold values from 0 to 1279, as said below
- counts: int32 [32], replicated, may hold values from 1 to 160, 3200 in all
- grad_out: bfloat16 [5120, 8192], P('seq', 'tp'), may hold values from -6 to 6
Outputs:
- branch_out: bfloat16 [5120, 8192], P('seq', 'tp')
- grad_queries: bfloat16 [5120, 8192], P('seq', 'tp')
- grad_keys_values: bfloat16 [2, 5120, 1024], P(None, 'seq', 'tp')
- grad_router: float32 [8192], P('tp')
The draws below stay inside these ranges and needn't reach their ends.
Inputs may be any that keep to these rules, and one draw needn't show every extreme that they name: Each row lists 160 different positions of one shard's tokens in increasing order; the first counts entries of a row are the shard's routed tokens. `counts`: each shard has at least one live slot and one shard has all 160.
All inputs are finite; a program needn't handle non-finite values.
Results may differ from the reference program's by a relative error of at most 0.03.
Values may be sent and summed in bfloat16 or wider, within the bound.
A program may use at most 128 MiB of HBM per device.

```python
import math
import jax
import jax.numpy as jnp
import numpy as np
from jax import lax

D = 8192
QUERY_HEADS = 64
HK = 8
HEAD_WIDTH = 128
TOK_DEV = 1280
SLOT_LIMIT = 160
SHARDS = 32
TOKENS = 40960
ROUTED = 5120


def draw_queries(key, part):
    result = jnp.clip(jax.random.normal(jax.random.fold_in(key, 1), (TOKENS, QUERY_HEADS * HEAD_WIDTH), jnp.float32), -6.0, 6.0)
    return result.astype(jnp.bfloat16)


def draw_keys_values(key, part):
    key_part = jnp.clip(jax.random.normal(jax.random.fold_in(key, 2), (TOKENS, HK * HEAD_WIDTH), jnp.float32), -6.0, 6.0)
    value_part = jnp.clip(jax.random.normal(jax.random.fold_in(key, 3), (TOKENS, HK * HEAD_WIDTH), jnp.float32), -6.0, 6.0)
    return jnp.stack([key_part, value_part]).astype(jnp.bfloat16)


def draw_routed(key, part):
    ranking = jax.random.randint(key, (SHARDS, TOK_DEV), 0, 2 ** 18) * TOK_DEV + jnp.arange(TOK_DEV, dtype=jnp.int32)[None, :]
    ranking = ranking.at[0, TOK_DEV - 1].set(2 ** 30)
    ranking = ranking.at[1, 0].set(2 ** 30)
    chosen = jax.lax.top_k(ranking, SLOT_LIMIT)[1]
    return jnp.sort(chosen, axis=1).astype(jnp.int32)


def shard_levels(key, shape, shards, smallest, top_value):
    level = 1.0
    for position, shards_of in shards:
        heights = jax.random.uniform(jax.random.fold_in(jax.random.fold_in(key, 6), position), (shards_of,), jnp.float32, smallest / len(shards), top_value / len(shards))
        level = level * jnp.repeat(jnp.exp(heights), shape[position] // shards_of).reshape((-1,) + (1,) * (len(shape) - 1 - position))
    return level


def split_up(count, total, bound, lean):
    portions = [(1 << 20) // math.isqrt(standing ** lean) + 1 for standing in range(2, count + 1)]
    rest, given = total - bound - (count - 1), [1] * (count - 1)
    while rest > 0:
        free = [i for i in range(count - 1) if given[i] < bound]
        pool, budget = sum([portions[i] for i in free]), rest
        for i in free:
            addition = min(bound - given[i], max(1, budget * portions[i] // pool), rest)
            given[i] = given[i] + addition
            rest = rest - addition
    return np.array([bound] + given)


def ragged(rng, number_of, total, bound, lean):
    if number_of == 2:
        one = jax.random.randint(rng, (), max(1, total - bound), min(bound, total - 1) + 1)
        return jnp.stack([one, total - one])
    sizes = jnp.asarray(split_up(number_of, total, bound, lean), jnp.int32)
    couples = (number_of - 1) // 2
    giver, receiver = sizes[1:1 + 2 * couples:2], sizes[2:2 + 2 * couples:2]
    room = jnp.minimum(giver - 1, bound - receiver)
    moved = jax.random.randint(jax.random.fold_in(rng, 1), (couples,), 0, 1 << 20) % (room + 1)
    sizes = sizes.at[1:1 + 2 * couples:2].set(giver - moved).at[2:2 + 2 * couples:2].set(receiver + moved)
    return sizes[jax.random.permutation(jax.random.fold_in(rng, 2), number_of)]


def centred(stream_key, dims, width, limit, cuts=(), held_as=jnp.bfloat16):
    array = jax.random.normal(stream_key, dims, jnp.float32) * width
    if len(cuts) > 0:
        array = shard_levels(stream_key, dims, cuts, -0.22, 0.18) * array
    return jnp.clip(array, min=-limit, max=limit).astype(held_as)


def setup_inputs(seed: int = 0) -> dict:
    splits = jax.random.split(jax.random.key(seed), 8)
    return {
        "hidden": centred(splits[0], (TOKENS, D), 1.0, 6.0, ((0, 32), (1, 8))),
        "queries": draw_queries(jax.random.fold_in(splits[7], 71), 0),
        "keys_values": draw_keys_values(jax.random.fold_in(splits[7], 71), 0),
        "w_router": centred(splits[3], (D,), D ** -0.5, 0.0625, ((0, 8),)),
        "routed": draw_routed(jax.random.fold_in(splits[7], 71), 0),
        "counts": ragged(splits[5], SHARDS, SHARDS * SLOT_LIMIT * 5 // 8, SLOT_LIMIT, 2).astype(jnp.int32),
        "grad_out": centred(splits[6], (ROUTED, QUERY_HEADS * HEAD_WIDTH), 1.0, 6.0, ((0, 32), (1, 8))),
    }


def reference(hidden, queries, keys_values, w_router, routed, counts, grad_out):
    group = QUERY_HEADS // HK
    logit_scale_factor = 1.0 / math.sqrt(HEAD_WIDTH)
    offsets = (jnp.arange(SHARDS, dtype=jnp.int32) * TOK_DEV)[:, None]
    positions = (routed.astype(jnp.int32) + offsets).reshape(-1)
    live_slots = (jnp.arange(SLOT_LIMIT, dtype=jnp.int32)[None, :] < counts[:, None]).reshape(-1)
    chosen_x = hidden[positions]
    logit = jnp.dot(chosen_x, w_router, preferred_element_type=jnp.float32)
    gate = jax.nn.sigmoid(logit)
    live_float = live_slots.astype(jnp.float32)
    weight_all = gate * live_float
    query_all = queries[positions].reshape(ROUTED, HK, group, HEAD_WIDTH).astype(jnp.float32)
    every_key = keys_values[0][positions].reshape(ROUTED, HK, HEAD_WIDTH).astype(jnp.float32)
    every_value = keys_values[1][positions].reshape(ROUTED, HK, HEAD_WIDTH).astype(jnp.float32)
    upstream_all = grad_out.astype(jnp.float32).reshape(ROUTED, HK, group, HEAD_WIDTH)
    slot_ids = jnp.arange(ROUTED, dtype=jnp.int32)

    def shard_step(carried, shard):
        key_gradient, value_gradient, router_acc = carried
        first_row = shard * SLOT_LIMIT
        routed_query_rows = lax.dynamic_slice_in_dim(query_all, first_row, SLOT_LIMIT, 0)
        upstream = lax.dynamic_slice_in_dim(upstream_all, first_row, SLOT_LIMIT, 0)
        weight_rows = lax.dynamic_slice_in_dim(weight_all, first_row, SLOT_LIMIT, 0)
        gate_rows = lax.dynamic_slice_in_dim(gate, first_row, SLOT_LIMIT, 0)
        live_rows = lax.dynamic_slice_in_dim(live_float, first_row, SLOT_LIMIT, 0)
        x_rows = lax.dynamic_slice_in_dim(chosen_x, first_row, SLOT_LIMIT, 0)
        query_slots = first_row + jnp.arange(SLOT_LIMIT, dtype=jnp.int32)
        allowed = (slot_ids[None, :] <= query_slots[:, None]) & live_slots[None, :]
        score_matrix = jnp.einsum('vemc,uec->emvu', routed_query_rows, every_key) * logit_scale_factor
        masked = jnp.where(allowed, score_matrix, -jnp.inf)
        row_max = lax.optimization_barrier(jnp.max(masked, axis=-1))
        lse = row_max + jnp.log(lax.optimization_barrier(jnp.sum(jnp.exp(masked - row_max[..., None]), axis=-1)))
        probs = jnp.exp(masked - lse[..., None])
        probs_narrow = lax.optimization_barrier(probs.astype(jnp.bfloat16)).astype(jnp.float32)
        attention_output = jnp.einsum('psot,tpn->opsn', probs_narrow, every_value)
        out_rows = (attention_output * weight_rows[:, None, None, None]).reshape(SLOT_LIMIT, QUERY_HEADS * HEAD_WIDTH).astype(jnp.bfloat16)
        gradient_rows = lax.optimization_barrier((upstream * weight_rows[:, None, None, None]).astype(jnp.bfloat16)).astype(jnp.float32)
        dlogit = lax.optimization_barrier(jnp.sum(upstream * attention_output, axis=(1, 2, 3))) * gate_rows * (1.0 - gate_rows) * live_rows
        delta = lax.optimization_barrier(jnp.sum(gradient_rows * attention_output, axis=-1)).transpose(1, 2, 0)
        prob_gradient = jnp.einsum('vemc,uec->emvu', gradient_rows, every_value)
        score_gradient = lax.optimization_barrier((probs * (prob_gradient - delta[..., None])).astype(jnp.bfloat16)).astype(jnp.float32)
        query_gradient = (jnp.einsum('psot,tpn->opsn', score_gradient, every_key) * logit_scale_factor).reshape(SLOT_LIMIT, QUERY_HEADS * HEAD_WIDTH).astype(jnp.bfloat16)
        key_gradient = key_gradient + jnp.einsum('cfym,ycfh->mch', score_gradient, routed_query_rows) * logit_scale_factor
        value_gradient = value_gradient + jnp.einsum('cfym,ycfh->mch', probs_narrow, gradient_rows)
        router_acc = router_acc + jnp.dot(dlogit, x_rows.astype(jnp.float32))
        return ((key_gradient, value_gradient, router_acc), (out_rows, query_gradient))
    start_carry = (jnp.zeros((ROUTED, HK, HEAD_WIDTH), jnp.float32), jnp.zeros((ROUTED, HK, HEAD_WIDTH), jnp.float32), jnp.zeros((D,), jnp.float32))
    final, stacked = lax.scan(shard_step, start_carry, jnp.arange(SHARDS, dtype=jnp.int32))
    key_gradient, value_gradient, router_acc = final
    branch_out = stacked[0].reshape(ROUTED, QUERY_HEADS * HEAD_WIDTH)
    grad_queries = stacked[1].reshape(ROUTED, QUERY_HEADS * HEAD_WIDTH)
    grad_keys_values = jnp.stack([key_gradient.reshape(ROUTED, HK * HEAD_WIDTH), value_gradient.reshape(ROUTED, HK * HEAD_WIDTH)]).astype(jnp.bfloat16)
    return (branch_out, grad_queries, grad_keys_values, router_acc)
```

```python
import functools
import math

import jax
import jax.numpy as jnp
from jax import lax
from jax.experimental import pallas as pl
from jax.experimental.pallas import tpu as pltpu
from jax.sharding import PartitionSpec as P

HEAD_WIDTH = 128
MESH = pl.DeviceIdType.MESH
NEG = -1e30
CHUNK = 256
LIVE_SHARE = (5, 8)
F32 = jnp.float32
BF16 = jnp.bfloat16


def dot_nn(a, b):
    return lax.dot_general(a, b, (((1,), (0,)), ((), ())), preferred_element_type=F32)


def dot_nt(a, b):
    return lax.dot_general(a, b, (((1,), (1,)), ((), ())), preferred_element_type=F32)


def dot_tn(a, b):
    return lax.dot_general(a, b, (((0,), (0,)), ((), ())), preferred_element_type=F32)


def rows_of(row, cap):
    return jnp.broadcast_to(row, (128, cap)).T


def fetch_kernel(nseq, ntp, hid, qry, kv, w, routed, x_out, q_out, kvall, logit_out,
                 hid_v, qry_v, kv_v, part, lsem, ssem, rsem, fsem, gsem, tssem, trsem):
    me, mt = lax.axis_index("seq"), lax.axis_index("tp")
    nchip = nseq // 2
    chip, core = me // 2, me % 2
    sib = me + 1 - 2 * core
    cap = routed.shape[1]
    tok = hid.shape[0]
    heads = q_out.shape[0]
    load_kv = pltpu.make_async_copy(kv, kv_v, lsem.at[0])
    load_hid = pltpu.make_async_copy(hid, hid_v, lsem.at[1])
    load_qry = pltpu.make_async_copy(qry, qry_v, lsem.at[2])
    load_kv.start()
    load_hid.start()
    load_qry.start()

    barrier = pltpu.get_barrier_semaphore()

    def greet_chip(c, _):
        @pl.when(c < chip)
        def _():
            pl.semaphore_signal(barrier, inc=1, device_id={"seq": 2 * c + core}, device_id_type=MESH)
        return 0

    def greet_tp(t, _):
        @pl.when(t != mt)
        def _():
            pl.semaphore_signal(barrier, inc=1, device_id={"tp": t}, device_id_type=MESH)
        return 0

    lax.fori_loop(0, nchip, greet_chip, 0)
    pl.semaphore_signal(barrier, inc=1, device_id={"seq": sib}, device_id_type=MESH)
    lax.fori_loop(0, ntp, greet_tp, 0)

    col = rows_of(routed[...].astype(F32), cap)
    lane = lax.broadcasted_iota(jnp.int32, (cap, 128), 1).astype(F32)
    onehot = jnp.concatenate(
        [jnp.where(col == lane + 128.0 * j, 1.0, 0.0).astype(BF16) for j in range(tok // 128)], axis=1
    )
    load_kv.wait()
    kvall[me, :, 0:128] = dot_nn(onehot, kv_v[0]).astype(BF16)
    kvall[me, :, 128:256] = dot_nn(onehot, kv_v[1]).astype(BF16)

    pl.semaphore_wait(barrier, nchip - 1 - chip + 1 + ntp - 1)

    def to_chip(c):
        return pltpu.make_async_remote_copy(
            src_ref=kvall.at[me], dst_ref=kvall.at[me], send_sem=ssem.at[c], recv_sem=rsem.at[chip],
            device_id={"seq": 2 * c + core}, device_id_type=MESH)

    def send_chip(i, _):
        c = nchip - 1 - i

        @pl.when(c > chip)
        def _():
            to_chip(c).start()
        return 0

    def own_to_sib():
        return pltpu.make_async_remote_copy(
            src_ref=kvall.at[me], dst_ref=kvall.at[me], send_sem=fsem.at[chip], recv_sem=gsem.at[chip],
            device_id={"seq": sib}, device_id_type=MESH)

    lax.fori_loop(0, nchip, send_chip, 0)

    @pl.when(core == 0)
    def _():
        own_to_sib().start()

    load_hid.wait()
    x = dot_nn(onehot, hid_v[...]).astype(BF16)
    x_out[...] = x
    logit = dot_nt(jnp.broadcast_to(w[...], (16, w.shape[1])), x)
    part[mt, :, :] = jnp.zeros((8, 256), F32)
    part[mt, :, 0:cap] = logit[0:8]

    def to_tp(t):
        return pltpu.make_async_remote_copy(
            src_ref=part.at[mt], dst_ref=part.at[mt], send_sem=tssem.at[t], recv_sem=trsem.at[mt],
            device_id={"tp": t}, device_id_type=MESH)

    def from_tp(t):
        return pltpu.make_async_remote_copy(
            src_ref=part.at[t], dst_ref=part.at[t], send_sem=tssem.at[t], recv_sem=trsem.at[t],
            device_id={"tp": t}, device_id_type=MESH)

    def send_tp(t, _):
        @pl.when(t != mt)
        def _():
            to_tp(t).start()
        return 0

    lax.fori_loop(0, ntp, send_tp, 0)

    load_qry.wait()
    for h in range(heads):
        q_out[h] = dot_nn(onehot, qry_v[:, h * 128:(h + 1) * 128]).astype(BF16)

    def wait_tp(t, _):
        @pl.when(t != mt)
        def _():
            from_tp(t).wait_recv()
        return 0

    lax.fori_loop(0, ntp, wait_tp, 0)
    total = part[0]
    for t in range(1, ntp):
        total = total + part[t]
    logit_out[...] = total

    def landed(c):
        block = kvall.at[2 * c + core]
        return pltpu.make_async_remote_copy(
            src_ref=block, dst_ref=block, send_sem=fsem.at[c], recv_sem=rsem.at[c],
            device_id={"seq": sib}, device_id_type=MESH)

    def forward(c):
        block = kvall.at[2 * c + core]
        return pltpu.make_async_remote_copy(
            src_ref=block, dst_ref=block, send_sem=fsem.at[c], recv_sem=gsem.at[c],
            device_id={"seq": sib}, device_id_type=MESH)

    def forwarded(c):
        block = kvall.at[2 * c + 1 - core]
        return pltpu.make_async_remote_copy(
            src_ref=block, dst_ref=block, send_sem=fsem.at[c], recv_sem=gsem.at[c],
            device_id={"seq": sib}, device_id_type=MESH)

    def pass_on(i, _):
        c = chip - 1 - i

        @pl.when(c >= 0)
        def _():
            landed(c).wait_recv()
            forward(c).start()
        return 0

    lax.fori_loop(0, nchip, pass_on, 0)

    def finish(c, _):
        @pl.when(c < chip)
        def _():
            forwarded(c).wait_recv()
            forward(c).wait_send()

        @pl.when(c > chip)
        def _():
            to_chip(c).wait_send()
        return 0

    lax.fori_loop(0, nchip, finish, 0)

    @pl.when(core == 0)
    def _():
        own_to_sib().wait_send()

    @pl.when(core == 1)
    def _():
        forwarded(chip).wait_recv()

    def finish_tp(t, _):
        @pl.when(t != mt)
        def _():
            to_tp(t).wait_send()
        return 0

    lax.fori_loop(0, ntp, finish_tp, 0)


def attend_kernel(scale, counts, kvall, q, g, logit, branch, dq, contrib, own, gterm,
                  kx, vx, qtx, dotx, dob, s_scr, e_scr, ot, wide, dkv):
    me = lax.axis_index("seq")
    cap, width = g.shape
    nq = q.shape[0]
    heads = width // 128
    to_exp2 = scale * math.log2(math.e)
    live_here = counts[me]

    row = lax.broadcasted_iota(jnp.int32, (cap, 128), 0)
    lane = lax.broadcasted_iota(jnp.int32, (cap, 128), 1)
    ones3 = jnp.where(lane < 3, 1.0, 0.0).astype(BF16)
    kx[0:cap, 0:128] = kvall[me, :, 0:128]
    kx[0:cap, 128:256] = jnp.zeros((cap, 128), BF16)
    vx[0:cap, 0:128] = kvall[me, :, 128:256]
    vx[0:cap, 128:256] = ones3

    def place(s, off):
        off = pl.multiple_of(off, 16)
        n = counts[s]
        kx[pl.ds(off, cap), 0:128] = kvall[s, :, 0:128]
        kx[pl.ds(off, cap), 128:256] = jnp.where((row >= n) & (lane == 0), NEG, 0.0).astype(BF16)
        vx[pl.ds(off, cap), 0:128] = kvall[s, :, 128:256]
        vx[pl.ds(off, cap), 128:256] = ones3
        return off + ((n + 15) // 16) * 16

    end = pl.multiple_of(lax.fori_loop(0, me, place, cap), 16)
    kx[pl.ds(end, CHUNK), 0:128] = jnp.zeros((CHUNK, 128), BF16)
    kx[pl.ds(end, CHUNK), 128:256] = jnp.where(
        lax.broadcasted_iota(jnp.int32, (CHUNK, 128), 1) == 0, NEG, 0.0).astype(BF16)
    vx[pl.ds(end, CHUNK), :] = jnp.zeros((CHUNK, 256), BF16)
    chunks = (end - cap + CHUNK - 1) // CHUNK

    def at(c):
        return pl.ds(pl.multiple_of(cap + c * CHUNK, 32), CHUNK)

    qtx[0:128, :] = q[...].T
    first = lax.broadcasted_iota(jnp.int32, (128, nq), 0)
    qtx[128:256, :] = jnp.where(first == 0, 1.0, 0.0).astype(BF16)

    key_slot = lax.broadcasted_iota(jnp.int32, (cap, nq), 0)
    pos = lax.broadcasted_iota(jnp.int32, (cap, nq), 1)
    query_slot = pos
    for h in range(1, heads):
        query_slot = query_slot - jnp.where(pos >= h * cap, cap, 0)
    s = jnp.where(key_slot <= query_slot, dot_nn(kx[0:cap, :], qtx[...]), NEG)
    s_scr[0:cap, :] = s
    top = jnp.max(s.reshape(cap // 8, 8, nq), axis=0)

    def score(c, top):
        s = dot_nn(kx[at(c), :], qtx[...])
        s_scr[at(c), :] = s
        return jnp.maximum(top, jnp.max(s.reshape(CHUNK // 8, 8, nq), axis=0))

    top = lax.fori_loop(0, chunks, score, top)
    top = jnp.max(top, axis=0, keepdims=True) * to_exp2

    def soften(sl, rows, total, start):
        e = jnp.exp2(s_scr[sl, :] * to_exp2 - top)
        eb = e.astype(BF16)
        e_scr[sl, :] = eb
        add = dot_tn(vx[sl, 0:128], eb)
        ot[...] = add if start else ot[...] + add
        return total + jnp.sum(e.reshape(rows // 8, 8, nq), axis=0)

    total = soften(pl.ds(0, cap), cap, jnp.zeros((8, nq), F32), True)
    total = lax.fori_loop(0, chunks, lambda c, t: soften(at(c), CHUNK, t, False), total)
    inverse = 1.0 / jnp.sum(total, axis=0, keepdims=True)

    z = logit[0:1, 0:cap]
    gate = 1.0 / (1.0 + jnp.exp(-z))
    live = lax.broadcasted_iota(jnp.int32, (1, cap), 1) < live_here
    weight = rows_of(jnp.where(live, gate, 0.0), cap)
    factor = jnp.where(live, gate * (1.0 - gate), 0.0)
    ot[...] = ot[...] * inverse
    wide[...] = ot[...].T
    acc = jnp.zeros((cap, 128), F32)
    for h in range(heads):
        rows, lanes = slice(h * cap, (h + 1) * cap), slice(h * 128, (h + 1) * 128)
        o = wide[rows, :]
        up = g[:, lanes].astype(F32)
        branch[:, lanes] = (o * weight).astype(BF16)
        acc = acc + up * o
        wide[rows, :] = up * weight
    gterm[0:8, :] = jnp.zeros((8, 256), F32)
    gterm[0:1, 0:cap] = jnp.sum(acc.T, axis=0, keepdims=True)
    gterm[1:2, 0:cap] = factor
    cot = (wide[...].T * inverse).astype(BF16)
    dotx[0:128, :] = cot
    cotf = cot.astype(F32)
    delta = -jnp.sum(cotf * ot[...], axis=0, keepdims=True)
    d1 = delta.astype(BF16).astype(F32)
    d2 = (delta - d1).astype(BF16).astype(F32)
    d3 = delta - d1 - d2
    dotx[128:256, :] = jnp.where(
        first == 0, d1, jnp.where(first == 1, d2, jnp.where(first == 2, d3, 0.0))).astype(BF16)
    dob[...] = cotf.T.astype(BF16)

    def back(sl, start):
        e = e_scr[sl, :]
        ds = (e.astype(F32) * dot_nn(vx[sl, :], dotx[...])).astype(BF16)
        add = dot_tn(kx[sl, 0:128], ds)
        wide_t = ot
        wide_t[...] = add if start else wide_t[...] + add
        return dot_nn(ds, q[...]) * scale, dot_nn(e, dob[...])

    dk, dv = back(pl.ds(0, cap), True)
    own[:, 0:128] = dk
    own[:, 128:256] = dv

    def back_chunk(c, _):
        dk, dv = back(at(c), False)
        dkv[at(c), 0:128] = dk.astype(BF16)
        dkv[at(c), 128:256] = dv.astype(BF16)
        return 0

    lax.fori_loop(0, chunks, back_chunk, 0)

    wide[...] = (ot[...] * scale).T
    for h in range(heads):
        dq[:, h * 128:(h + 1) * 128] = wide[h * cap:(h + 1) * cap, :].astype(BF16)

    row2 = lax.broadcasted_iota(jnp.int32, (cap, 256), 0)

    def unplace(s, off):
        off = pl.multiple_of(off, 16)
        n = counts[s]
        block = dkv[pl.ds(off, cap), :].astype(F32)
        contrib[s % 2, s // 2] = jnp.where(row2 < n, block, 0.0).astype(BF16)
        return off + ((n + 15) // 16) * 16

    lax.fori_loop(0, me, unplace, cap)


def return_kernel(nseq, ntp, contrib, own, gterm, x, dkv_out, router_out,
                  pair, mine, inbox, part, gpair, gchip, sums, psem, prsem, ssem, rsem, tssem, trsem,
                  qsem, qrsem, gssem, grsem):
    me, mt = lax.axis_index("seq"), lax.axis_index("tp")
    nchip = nseq // 2
    chip, core = me // 2, me % 2
    sib = me + 1 - 2 * core
    cap = x.shape[0]

    barrier = pltpu.get_barrier_semaphore()

    def greet_chip(c, _):
        @pl.when(c != chip)
        def _():
            pl.semaphore_signal(barrier, inc=1, device_id={"seq": 2 * c + core}, device_id_type=MESH)
        return 0

    def greet_tp(t, _):
        @pl.when(t != mt)
        def _():
            pl.semaphore_signal(barrier, inc=1, device_id={"tp": t}, device_id_type=MESH)
        return 0

    lax.fori_loop(0, nchip, greet_chip, 0)
    pl.semaphore_signal(barrier, inc=1, device_id={"seq": sib}, device_id_type=MESH)
    lax.fori_loop(0, ntp, greet_tp, 0)
    part[mt] = gterm[...]
    pl.semaphore_wait(barrier, nchip - 1 + 1 + ntp - 1)

    def tp_copy(slot, t):
        return pltpu.make_async_remote_copy(
            src_ref=part.at[slot], dst_ref=part.at[slot], send_sem=tssem.at[t], recv_sem=trsem.at[slot],
            device_id={"tp": t}, device_id_type=MESH)

    def send_tp(t, _):
        @pl.when(t != mt)
        def _():
            tp_copy(mt, t).start()
        return 0

    lax.fori_loop(0, ntp, send_tp, 0)

    def pair_copy(c):
        return pltpu.make_async_remote_copy(
            src_ref=contrib.at[1 - core, c], dst_ref=pair.at[c], send_sem=psem.at[c], recv_sem=prsem.at[c],
            device_id={"seq": sib}, device_id_type=MESH)

    def send_pair(c, _):
        @pl.when((c < chip) | ((c == chip) & (core == 1)))
        def _():
            pair_copy(c).start()
        return 0

    lax.fori_loop(0, nchip, send_pair, 0)

    def chip_copy(c):
        return pltpu.make_async_remote_copy(
            src_ref=mine.at[c], dst_ref=inbox.at[chip], send_sem=ssem.at[c], recv_sem=rsem.at[chip],
            device_id={"seq": 2 * c + core}, device_id_type=MESH)

    def join(c, _):
        @pl.when(c < chip)
        def _():
            pair_copy(c).wait_recv()
            mine[c] = (contrib[core, c].astype(F32) + pair[c].astype(F32)).astype(BF16)
            chip_copy(c).start()
        return 0

    lax.fori_loop(0, nchip, join, 0)

    def wait_tp(t, _):
        @pl.when(t != mt)
        def _():
            tp_copy(t, t).wait_recv()
        return 0

    lax.fori_loop(0, ntp, wait_tp, 0)
    total = part[0, 0:1, :]
    for t in range(1, ntp):
        total = total + part[t, 0:1, :]
    dlogit = (total * gterm[1:2, :])[:, 0:cap]
    p1 = dlogit.astype(BF16)
    r1 = dlogit - p1.astype(F32)
    p2 = r1.astype(BF16)
    p3 = (r1 - p2.astype(F32)).astype(BF16)
    xs = x[...]
    share = (dot_nn(jnp.broadcast_to(p1, (16, cap)), xs) + dot_nn(jnp.broadcast_to(p2, (16, cap)), xs)
             + dot_nn(jnp.broadcast_to(p3, (16, cap)), xs))
    for i in range(8):
        gpair[core, i:i + 1, :] = share[0:1, i * 128:(i + 1) * 128]

    def gpair_copy(slot):
        return pltpu.make_async_remote_copy(
            src_ref=gpair.at[slot], dst_ref=gpair.at[slot], send_sem=qsem, recv_sem=qrsem,
            device_id={"seq": sib}, device_id_type=MESH)

    gpair_copy(core).start()
    gpair_copy(1 - core).wait_recv()
    gchip[chip] = gpair[0] + gpair[1]

    def gchip_copy(slot, c):
        return pltpu.make_async_remote_copy(
            src_ref=gchip.at[slot], dst_ref=gchip.at[slot], send_sem=gssem.at[c], recv_sem=grsem.at[slot],
            device_id={"seq": 2 * c + core}, device_id_type=MESH)

    def send_gchip(c, _):
        @pl.when(c != chip)
        def _():
            gchip_copy(chip, c).start()
        return 0

    lax.fori_loop(0, nchip, send_gchip, 0)

    @pl.when(core == 0)
    def _():
        pair_copy(chip).wait_recv()
        pair[nchip] = pair[chip]

    @pl.when(core == 1)
    def _():
        pair[nchip] = jnp.zeros((cap, 256), BF16)

    def inbox_copy(c):
        return pltpu.make_async_remote_copy(
            src_ref=inbox.at[c], dst_ref=inbox.at[c], send_sem=ssem.at[c], recv_sem=rsem.at[c],
            device_id={"seq": 2 * c + core}, device_id_type=MESH)

    sums[...] = own[...] + pair[nchip].astype(F32)

    def add(c, _):
        @pl.when(c > chip)
        def _():
            inbox_copy(c).wait_recv()
            sums[...] = sums[...] + inbox[c].astype(F32)
        return 0

    lax.fori_loop(0, nchip, add, 0)
    dkv_out[0] = sums[:, 0:128].astype(BF16)
    dkv_out[1] = sums[:, 128:256].astype(BF16)

    def wait_gchip(c, _):
        @pl.when(c != chip)
        def _():
            gchip_copy(c, c).wait_recv()
        return 0

    lax.fori_loop(0, nchip, wait_gchip, 0)
    total = gchip[0]
    for c in range(1, nchip):
        total = total + gchip[c]
    router_out[...] = total

    gpair_copy(core).wait_send()

    def finish(c, _):
        @pl.when((c < chip) | ((c == chip) & (core == 1)))
        def _():
            pair_copy(c).wait_send()

        @pl.when(c < chip)
        def _():
            chip_copy(c).wait_send()

        @pl.when(c != chip)
        def _():
            gchip_copy(chip, c).wait_send()
        return 0

    lax.fori_loop(0, nchip, finish, 0)

    def finish_tp(t, _):
        @pl.when(t != mt)
        def _():
            tp_copy(mt, t).wait_send()
        return 0

    lax.fori_loop(0, ntp, finish_tp, 0)


def vmem(n=1):
    specs = [pl.BlockSpec(memory_space=pltpu.VMEM) for _ in range(n)]
    return specs if n > 1 else specs[0]


def shards(hidden, queries, keys_values, w_router, routed, counts, grad_out):
    nseq, ntp = lax.axis_size("seq"), lax.axis_size("tp")
    nchip = nseq // 2
    cap = routed.shape[1]
    tok, width = queries.shape
    heads = width // HEAD_WIDTH
    nq = heads * cap
    scale = 1.0 / math.sqrt(HEAD_WIDTH)
    dma, shape = pltpu.SemaphoreType.DMA, jax.ShapeDtypeStruct
    anywhere = pl.BlockSpec(memory_space=pl.ANY)

    x, q, kvall, logit = pl.pallas_call(
        functools.partial(fetch_kernel, nseq, ntp),
        out_shape=(shape((cap, width), BF16), shape((heads, cap, 128), BF16),
                   shape((nseq, cap, 256), BF16), shape((8, 256), F32)),
        in_specs=[anywhere] * 3 + vmem(2),
        out_specs=tuple(vmem(4)),
        scratch_shapes=[
            pltpu.VMEM((tok, width), BF16), pltpu.VMEM((tok, width), BF16), pltpu.VMEM((2, tok, 128), BF16),
            pltpu.VMEM((ntp, 8, 256), F32), dma((3,)), dma((nchip,)), dma((nchip,)), dma((nchip,)),
            dma((nchip,)), dma((ntp,)), dma((ntp,)),
        ],
        compiler_params=pltpu.CompilerParams(
            collective_id=0, has_side_effects=True, vmem_limit_bytes=40 * 2 ** 20),
        name="fetch",
    )(hidden, queries, keys_values, w_router.reshape(1, width), routed)

    live = nseq * cap * LIVE_SHARE[0] // LIVE_SHARE[1]
    span = -(-(live + 15 * nseq) // CHUNK) * CHUNK
    rows = cap + span + CHUNK
    branch, dq, contrib, own, gterm = pl.pallas_call(
        functools.partial(attend_kernel, scale),
        out_shape=(shape((cap, width), BF16), shape((cap, width), BF16),
                   shape((2, nchip, cap, 256), BF16), shape((cap, 256), F32), shape((8, 256), F32)),
        in_specs=[pl.BlockSpec(memory_space=pltpu.SMEM)] + vmem(4),
        out_specs=tuple(vmem(5)),
        scratch_shapes=[
            pltpu.VMEM((rows, 256), BF16), pltpu.VMEM((rows, 256), BF16),
            pltpu.VMEM((256, nq), BF16), pltpu.VMEM((256, nq), BF16), pltpu.VMEM((nq, 128), BF16),
            pltpu.VMEM((cap + span, nq), F32), pltpu.VMEM((cap + span, nq), BF16),
            pltpu.VMEM((128, nq), F32), pltpu.VMEM((nq, 128), F32), pltpu.VMEM((rows, 256), BF16),
        ],
        compiler_params=pltpu.CompilerParams(vmem_limit_bytes=60 * 2 ** 20),
        name="attend",
    )(counts, kvall, q.reshape(nq, 128), grad_out, logit)

    dkv, router = pl.pallas_call(
        functools.partial(return_kernel, nseq, ntp),
        out_shape=(shape((2, cap, 128), BF16), shape((8, 128), F32)),
        in_specs=vmem(4),
        out_specs=tuple(vmem(2)),
        scratch_shapes=[
            pltpu.VMEM((nchip + 1, cap, 256), BF16), pltpu.VMEM((nchip, cap, 256), BF16),
            pltpu.VMEM((nchip, cap, 256), BF16), pltpu.VMEM((ntp, 8, 256), F32),
            pltpu.VMEM((2, 8, 128), F32), pltpu.VMEM((nchip, 8, 128), F32), pltpu.VMEM((cap, 256), F32),
            dma((nchip,)), dma((nchip,)), dma((nchip,)), dma((nchip,)), dma((ntp,)), dma((ntp,)),
            dma, dma, dma((nchip,)), dma((nchip,)),
        ],
        compiler_params=pltpu.CompilerParams(
            collective_id=1, has_side_effects=True, vmem_limit_bytes=40 * 2 ** 20),
        name="settle",
    )(contrib, own, gterm, x)
    return branch, dq, dkv, router.reshape(8 * 128)


def solution(mesh):
    in_specs = (
        P("seq", "tp"),
        P("seq", "tp"),
        P(None, "seq", "tp"),
        P("tp"),
        P("seq", None),
        P(),
        P("seq", "tp"),
    )
    out_specs = (P("seq", "tp"), P("seq", "tp"), P(None, "seq", "tp"), P("tp"))
    return jax.shard_map(shards, mesh=mesh, in_specs=in_specs, out_specs=out_specs, check_vma=False)
```

```python
import functools
import math

import jax
import jax.numpy as jnp
from jax import lax
from jax.experimental import pallas as pl
from jax.experimental.pallas import tpu as pltpu
from jax.sharding import PartitionSpec as P

HEAD_WIDTH = 128
MESH = pl.DeviceIdType.MESH
NEG = -1e30
VMEM_LIMIT = 62 * 2 ** 20
CHUNK = 256
LIVE_SHARE = (5, 8)
F32 = jnp.float32
BF16 = jnp.bfloat16


def dot_nn(a, b):
    return lax.dot_general(a, b, (((1,), (0,)), ((), ())), preferred_element_type=F32)


def dot_nt(a, b):
    return lax.dot_general(a, b, (((1,), (1,)), ((), ())), preferred_element_type=F32)


def dot_tn(a, b):
    return lax.dot_general(a, b, (((0,), (0,)), ((), ())), preferred_element_type=F32)


def rows_of(row, cap):
    return jnp.broadcast_to(row, (128, cap)).T


def fetch_kernel(nseq, ntp, hid, qry, kv, w, routed, x_out, q_out, kvall, logit_out,
                 hid_v, qry_v, kv_v, held, part, lsem, ssem, rsem, fsem, gsem, tssem, trsem):
    me, mt = lax.axis_index("seq"), lax.axis_index("tp")
    nchip = nseq // 2
    chip, core = me // 2, me % 2
    sib = me + 1 - 2 * core
    cap = routed.shape[1]
    tok = hid.shape[0]
    heads = q_out.shape[0]
    load_kv = pltpu.make_async_copy(kv, kv_v, lsem.at[0])
    load_hid = pltpu.make_async_copy(hid, hid_v, lsem.at[1])
    load_qry = pltpu.make_async_copy(qry, qry_v, lsem.at[2])
    load_kv.start()
    load_hid.start()
    load_qry.start()

    barrier = pltpu.get_barrier_semaphore()

    def greet_chip(c, _):
        @pl.when(c < chip)
        def _():
            pl.semaphore_signal(barrier, inc=1, device_id={"seq": 2 * c + core}, device_id_type=MESH)
        return 0

    def greet_tp(t, _):
        @pl.when(t != mt)
        def _():
            pl.semaphore_signal(barrier, inc=1, device_id={"tp": t}, device_id_type=MESH)
        return 0

    lax.fori_loop(0, nchip, greet_chip, 0)
    pl.semaphore_signal(barrier, inc=1, device_id={"seq": sib}, device_id_type=MESH)
    lax.fori_loop(0, ntp, greet_tp, 0)

    col = rows_of(routed[...].astype(F32), cap)
    lane = lax.broadcasted_iota(jnp.int32, (cap, 128), 1).astype(F32)
    onehot = jnp.concatenate(
        [jnp.where(col == lane + 128.0 * j, 1.0, 0.0).astype(BF16) for j in range(tok // 128)], axis=1
    )
    load_kv.wait()
    held[:, 0:128] = dot_nn(onehot, kv_v[0]).astype(BF16)
    held[:, 128:256] = dot_nn(onehot, kv_v[1]).astype(BF16)
    keep = pltpu.make_async_copy(held, kvall.at[me], lsem.at[3])
    keep.start()

    pl.semaphore_wait(barrier, nchip - 1 - chip + 1 + ntp - 1)

    def to_chip(c):
        return pltpu.make_async_remote_copy(
            src_ref=held, dst_ref=kvall.at[me], send_sem=ssem.at[c], recv_sem=rsem.at[chip],
            device_id={"seq": 2 * c + core}, device_id_type=MESH)

    def send_chip(i, _):
        c = nchip - 1 - i

        @pl.when(c > chip)
        def _():
            to_chip(c).start()
        return 0

    def own_to_sib():
        return pltpu.make_async_remote_copy(
            src_ref=held, dst_ref=kvall.at[me], send_sem=fsem.at[chip], recv_sem=gsem.at[chip],
            device_id={"seq": sib}, device_id_type=MESH)

    lax.fori_loop(0, nchip, send_chip, 0)

    @pl.when(core == 0)
    def _():
        own_to_sib().start()

    load_hid.wait()
    x = dot_nn(onehot, hid_v[...]).astype(BF16)
    x_out[...] = x
    logit = dot_nt(jnp.broadcast_to(w[...], (16, w.shape[1])), x)
    part[mt, :, :] = jnp.zeros((8, 256), F32)
    part[mt, :, 0:cap] = logit[0:8]

    def to_tp(t):
        return pltpu.make_async_remote_copy(
            src_ref=part.at[mt], dst_ref=part.at[mt], send_sem=tssem.at[t], recv_sem=trsem.at[mt],
            device_id={"tp": t}, device_id_type=MESH)

    def from_tp(t):
        return pltpu.make_async_remote_copy(
            src_ref=part.at[t], dst_ref=part.at[t], send_sem=tssem.at[t], recv_sem=trsem.at[t],
            device_id={"tp": t}, device_id_type=MESH)

    def send_tp(t, _):
        @pl.when(t != mt)
        def _():
            to_tp(t).start()
        return 0

    lax.fori_loop(0, ntp, send_tp, 0)

    load_qry.wait()
    for h in range(heads):
        q_out[h] = dot_nn(onehot, qry_v[:, h * 128:(h + 1) * 128]).astype(BF16)

    def wait_tp(t, _):
        @pl.when(t != mt)
        def _():
            from_tp(t).wait_recv()
        return 0

    lax.fori_loop(0, ntp, wait_tp, 0)
    total = part[0]
    for t in range(1, ntp):
        total = total + part[t]
    logit_out[...] = total

    def landed(c):
        block = kvall.at[2 * c + core]
        return pltpu.make_async_remote_copy(
            src_ref=block, dst_ref=block, send_sem=fsem.at[c], recv_sem=rsem.at[c],
            device_id={"seq": sib}, device_id_type=MESH)

    def forward(c):
        block = kvall.at[2 * c + core]
        return pltpu.make_async_remote_copy(
            src_ref=block, dst_ref=block, send_sem=fsem.at[c], recv_sem=gsem.at[c],
            device_id={"seq": sib}, device_id_type=MESH)

    def forwarded(c):
        block = kvall.at[2 * c + 1 - core]
        return pltpu.make_async_remote_copy(
            src_ref=block, dst_ref=block, send_sem=fsem.at[c], recv_sem=gsem.at[c],
            device_id={"seq": sib}, device_id_type=MESH)

    def pass_on(i, _):
        c = chip - 1 - i

        @pl.when(c >= 0)
        def _():
            landed(c).wait_recv()
            forward(c).start()
        return 0

    lax.fori_loop(0, nchip, pass_on, 0)

    def finish(c, _):
        @pl.when(c < chip)
        def _():
            forwarded(c).wait_recv()
            forward(c).wait_send()

        @pl.when(c > chip)
        def _():
            to_chip(c).wait_send()
        return 0

    lax.fori_loop(0, nchip, finish, 0)
    keep.wait()

    @pl.when(core == 0)
    def _():
        own_to_sib().wait_send()

    @pl.when(core == 1)
    def _():
        forwarded(chip).wait_recv()

    def finish_tp(t, _):
        @pl.when(t != mt)
        def _():
            to_tp(t).wait_send()
        return 0

    lax.fori_loop(0, ntp, finish_tp, 0)


def attend_kernel(scale, counts, kv_hbm, q_hbm, g_hbm, logit, branch, dq, contrib_hbm, own, gterm,
                  kvall, q, g, contrib, lsem, csem, kx, vx, qtx, dotx, dob, s_scr, e_scr, ot, wide, dkv):
    me = lax.axis_index("seq")
    cap, width = g.shape
    nq = q.shape[0]
    heads = width // 128
    to_exp2 = scale * math.log2(math.e)
    live_here = counts[me]
    loads = [
        pltpu.make_async_copy(kv_hbm.at[me], kvall.at[me], lsem.at[0]),
        pltpu.make_async_copy(q_hbm, q, lsem.at[1]),
        pltpu.make_async_copy(g_hbm, g, lsem.at[2]),
    ]
    for load in loads:
        load.start()

    def block_load(s):
        return pltpu.make_async_copy(kv_hbm.at[s], kvall.at[s], csem.at[s])

    def start_load(s, _):
        block_load(s).start()
        return 0

    lax.fori_loop(0, me, start_load, 0)

    row = lax.broadcasted_iota(jnp.int32, (cap, 128), 0)
    lane = lax.broadcasted_iota(jnp.int32, (cap, 128), 1)
    ones3 = jnp.where(lane < 3, 1.0, 0.0).astype(BF16)
    loads[0].wait()
    kx[0:cap, 0:128] = kvall[me, :, 0:128]
    kx[0:cap, 128:256] = jnp.zeros((cap, 128), BF16)
    vx[0:cap, 0:128] = kvall[me, :, 128:256]
    vx[0:cap, 128:256] = ones3

    def place(s, off):
        block_load(s).wait()
        off = pl.multiple_of(off, 16)
        n = counts[s]
        kx[pl.ds(off, cap), 0:128] = kvall[s, :, 0:128]
        kx[pl.ds(off, cap), 128:256] = jnp.where((row >= n) & (lane == 0), NEG, 0.0).astype(BF16)
        vx[pl.ds(off, cap), 0:128] = kvall[s, :, 128:256]
        vx[pl.ds(off, cap), 128:256] = ones3
        return off + ((n + 15) // 16) * 16

    end = pl.multiple_of(lax.fori_loop(0, me, place, cap), 16)
    kx[pl.ds(end, CHUNK), 0:128] = jnp.zeros((CHUNK, 128), BF16)
    kx[pl.ds(end, CHUNK), 128:256] = jnp.where(
        lax.broadcasted_iota(jnp.int32, (CHUNK, 128), 1) == 0, NEG, 0.0).astype(BF16)
    vx[pl.ds(end, CHUNK), :] = jnp.zeros((CHUNK, 256), BF16)
    chunks = (end - cap + CHUNK - 1) // CHUNK
    doubles = chunks // 2

    def at(c, size):
        return pl.ds(pl.multiple_of(cap + c * CHUNK, 32), size * CHUNK)

    def sweep(step, carry):
        carry = lax.fori_loop(0, doubles, lambda c, held: step(at(2 * c, 2), 2 * CHUNK, held), carry)
        return lax.fori_loop(2 * doubles, chunks, lambda c, held: step(at(c, 1), CHUNK, held), carry)

    loads[1].wait()

    qtx[0:128, :] = q[...].T
    first = lax.broadcasted_iota(jnp.int32, (128, nq), 0)
    qtx[128:256, :] = jnp.where(first == 0, 1.0, 0.0).astype(BF16)

    key_slot = lax.broadcasted_iota(jnp.int32, (cap, nq), 0)
    pos = lax.broadcasted_iota(jnp.int32, (cap, nq), 1)
    query_slot = pos
    for h in range(1, heads):
        query_slot = query_slot - jnp.where(pos >= h * cap, cap, 0)
    s = jnp.where(key_slot <= query_slot, dot_nn(kx[0:cap, :], qtx[...]), NEG)
    s_scr[0:cap, :] = s
    top = jnp.max(s.reshape(cap // 8, 8, nq), axis=0)

    def score(sl, rows, top):
        s = dot_nn(kx[sl, :], qtx[...])
        s_scr[sl, :] = s
        return jnp.maximum(top, jnp.max(s.reshape(rows // 8, 8, nq), axis=0))

    top = sweep(score, top)
    top = jnp.max(top, axis=0, keepdims=True) * to_exp2

    def soften(sl, rows, total, start):
        e = jnp.exp2(s_scr[sl, :] * to_exp2 - top)
        eb = e.astype(BF16)
        e_scr[sl, :] = eb
        add = dot_tn(vx[sl, 0:128], eb)
        ot[...] = add if start else ot[...] + add
        return total + jnp.sum(e.reshape(rows // 8, 8, nq), axis=0)

    total = soften(pl.ds(0, cap), cap, jnp.zeros((8, nq), F32), True)
    total = sweep(lambda sl, rows, t: soften(sl, rows, t, False), total)
    inverse = 1.0 / jnp.sum(total, axis=0, keepdims=True)

    z = logit[0:1, 0:cap]
    gate = 1.0 / (1.0 + jnp.exp(-z))
    live = lax.broadcasted_iota(jnp.int32, (1, cap), 1) < live_here
    weight = rows_of(jnp.where(live, gate, 0.0), cap)
    factor = jnp.where(live, gate * (1.0 - gate), 0.0)
    ot[...] = ot[...] * inverse
    wide[...] = ot[...].T
    loads[2].wait()
    acc = jnp.zeros((cap, 128), F32)
    for h in range(heads):
        rows, lanes = slice(h * cap, (h + 1) * cap), slice(h * 128, (h + 1) * 128)
        o = wide[rows, :]
        up = g[:, lanes].astype(F32)
        branch[:, lanes] = (o * weight).astype(BF16)
        acc = acc + up * o
        wide[rows, :] = up * weight
    gterm[0:8, :] = jnp.zeros((8, 256), F32)
    gterm[0:1, 0:cap] = jnp.sum(acc.T, axis=0, keepdims=True)
    gterm[1:2, 0:cap] = factor
    cot = (wide[...].T * inverse).astype(BF16)
    dotx[0:128, :] = cot
    cotf = cot.astype(F32)
    delta = -jnp.sum(cotf * ot[...], axis=0, keepdims=True)
    d1 = delta.astype(BF16).astype(F32)
    d2 = (delta - d1).astype(BF16).astype(F32)
    d3 = delta - d1 - d2
    dotx[128:256, :] = jnp.where(
        first == 0, d1, jnp.where(first == 1, d2, jnp.where(first == 2, d3, 0.0))).astype(BF16)
    dob[...] = cotf.T.astype(BF16)

    def back(sl, start):
        e = e_scr[sl, :]
        ds = e * dot_nn(vx[sl, :], dotx[...]).astype(BF16)
        add = dot_tn(kx[sl, 0:128], ds)
        wide_t = ot
        wide_t[...] = add if start else wide_t[...] + add
        return dot_nn(ds, q[...]) * scale, dot_nn(e, dob[...])

    dk, dv = back(pl.ds(0, cap), True)
    own[:, 0:128] = dk
    own[:, 128:256] = dv

    def back_chunk(sl, rows, _):
        dk, dv = back(sl, False)
        dkv[sl, 0:128] = dk.astype(BF16)
        dkv[sl, 128:256] = dv.astype(BF16)
        return 0

    sweep(back_chunk, 0)
    row2 = lax.broadcasted_iota(jnp.int32, (cap, 256), 0)

    def block_store(s):
        return pltpu.make_async_copy(contrib.at[s % 2, s // 2], contrib_hbm.at[s % 2, s // 2], csem.at[s])

    def unplace(s, off):
        off = pl.multiple_of(off, 16)
        n = counts[s]
        block = dkv[pl.ds(off, cap), :].astype(F32)
        contrib[s % 2, s // 2] = jnp.where(row2 < n, block, 0.0).astype(BF16)
        block_store(s).start()
        return off + ((n + 15) // 16) * 16

    lax.fori_loop(0, me, unplace, cap)

    wide[...] = (ot[...] * scale).T
    for h in range(heads):
        dq[:, h * 128:(h + 1) * 128] = wide[h * cap:(h + 1) * cap, :].astype(BF16)

    def finish_store(s, _):
        block_store(s).wait()
        return 0

    lax.fori_loop(0, me, finish_store, 0)


def return_kernel(nseq, ntp, contrib, own_hbm, gterm, x_hbm, dkv_out, router_out,
                  half, own, x, lsem, pair, mine, inbox, part, gpair, gchip, sums, psem, prsem, ssem, rsem, tssem, trsem,
                  qsem, qrsem, gssem, grsem):
    me, mt = lax.axis_index("seq"), lax.axis_index("tp")
    nchip = nseq // 2
    chip, core = me // 2, me % 2
    sib = me + 1 - 2 * core
    cap = x.shape[0]
    loads = [
        pltpu.make_async_copy(contrib.at[core], half, lsem.at[0]),
        pltpu.make_async_copy(own_hbm, own, lsem.at[1]),
        pltpu.make_async_copy(x_hbm, x, lsem.at[2]),
    ]
    for load in loads:
        load.start()

    barrier = pltpu.get_barrier_semaphore()

    def greet_chip(c, _):
        @pl.when(c != chip)
        def _():
            pl.semaphore_signal(barrier, inc=1, device_id={"seq": 2 * c + core}, device_id_type=MESH)
        return 0

    def greet_tp(t, _):
        @pl.when(t != mt)
        def _():
            pl.semaphore_signal(barrier, inc=1, device_id={"tp": t}, device_id_type=MESH)
        return 0

    lax.fori_loop(0, nchip, greet_chip, 0)
    pl.semaphore_signal(barrier, inc=1, device_id={"seq": sib}, device_id_type=MESH)
    lax.fori_loop(0, ntp, greet_tp, 0)
    part[mt] = gterm[...]
    pl.semaphore_wait(barrier, nchip - 1 + 1 + ntp - 1)

    def tp_copy(slot, t):
        return pltpu.make_async_remote_copy(
            src_ref=part.at[slot], dst_ref=part.at[slot], send_sem=tssem.at[t], recv_sem=trsem.at[slot],
            device_id={"tp": t}, device_id_type=MESH)

    def send_tp(t, _):
        @pl.when(t != mt)
        def _():
            tp_copy(mt, t).start()
        return 0

    lax.fori_loop(0, ntp, send_tp, 0)

    def pair_copy(c):
        return pltpu.make_async_remote_copy(
            src_ref=contrib.at[1 - core, c], dst_ref=pair.at[c], send_sem=psem.at[c], recv_sem=prsem.at[c],
            device_id={"seq": sib}, device_id_type=MESH)

    def send_pair(c, _):
        @pl.when((c < chip) | ((c == chip) & (core == 1)))
        def _():
            pair_copy(c).start()
        return 0

    lax.fori_loop(0, nchip, send_pair, 0)

    def chip_copy(c):
        return pltpu.make_async_remote_copy(
            src_ref=mine.at[c], dst_ref=inbox.at[chip], send_sem=ssem.at[c], recv_sem=rsem.at[chip],
            device_id={"seq": 2 * c + core}, device_id_type=MESH)

    loads[0].wait()

    def join(c, _):
        @pl.when(c < chip)
        def _():
            pair_copy(c).wait_recv()
            mine[c] = (half[c].astype(F32) + pair[c].astype(F32)).astype(BF16)
            chip_copy(c).start()
        return 0

    lax.fori_loop(0, nchip, join, 0)

    def wait_tp(t, _):
        @pl.when(t != mt)
        def _():
            tp_copy(t, t).wait_recv()
        return 0

    lax.fori_loop(0, ntp, wait_tp, 0)
    total = part[0, 0:1, :]
    for t in range(1, ntp):
        total = total + part[t, 0:1, :]
    dlogit = (total * gterm[1:2, :])[:, 0:cap]
    p1 = dlogit.astype(BF16)
    r1 = dlogit - p1.astype(F32)
    p2 = r1.astype(BF16)
    p3 = (r1 - p2.astype(F32)).astype(BF16)
    loads[2].wait()
    xs = x[...]
    share = (dot_nn(jnp.broadcast_to(p1, (16, cap)), xs) + dot_nn(jnp.broadcast_to(p2, (16, cap)), xs)
             + dot_nn(jnp.broadcast_to(p3, (16, cap)), xs))
    for i in range(8):
        gpair[core, i:i + 1, :] = share[0:1, i * 128:(i + 1) * 128]

    def gpair_copy(slot):
        return pltpu.make_async_remote_copy(
            src_ref=gpair.at[slot], dst_ref=gpair.at[slot], send_sem=qsem, recv_sem=qrsem,
            device_id={"seq": sib}, device_id_type=MESH)

    gpair_copy(core).start()
    gpair_copy(1 - core).wait_recv()
    gchip[chip] = gpair[0] + gpair[1]

    def gchip_copy(slot, c):
        return pltpu.make_async_remote_copy(
            src_ref=gchip.at[slot], dst_ref=gchip.at[slot], send_sem=gssem.at[c], recv_sem=grsem.at[slot],
            device_id={"seq": 2 * c + core}, device_id_type=MESH)

    def send_gchip(c, _):
        @pl.when(c != chip)
        def _():
            gchip_copy(chip, c).start()
        return 0

    lax.fori_loop(0, nchip, send_gchip, 0)

    @pl.when(core == 0)
    def _():
        pair_copy(chip).wait_recv()
        pair[nchip] = pair[chip]

    @pl.when(core == 1)
    def _():
        pair[nchip] = jnp.zeros((cap, 256), BF16)

    def inbox_copy(c):
        return pltpu.make_async_remote_copy(
            src_ref=inbox.at[c], dst_ref=inbox.at[c], send_sem=ssem.at[c], recv_sem=rsem.at[c],
            device_id={"seq": 2 * c + core}, device_id_type=MESH)

    loads[1].wait()
    sums[...] = own[...] + pair[nchip].astype(F32)

    def add(c, _):
        @pl.when(c > chip)
        def _():
            inbox_copy(c).wait_recv()
            sums[...] = sums[...] + inbox[c].astype(F32)
        return 0

    lax.fori_loop(0, nchip, add, 0)
    dkv_out[0] = sums[:, 0:128].astype(BF16)
    dkv_out[1] = sums[:, 128:256].astype(BF16)

    def wait_gchip(c, _):
        @pl.when(c != chip)
        def _():
            gchip_copy(c, c).wait_recv()
        return 0

    lax.fori_loop(0, nchip, wait_gchip, 0)
    total = gchip[0]
    for c in range(1, nchip):
        total = total + gchip[c]
    router_out[...] = total

    gpair_copy(core).wait_send()

    def finish(c, _):
        @pl.when((c < chip) | ((c == chip) & (core == 1)))
        def _():
            pair_copy(c).wait_send()

        @pl.when(c < chip)
        def _():
            chip_copy(c).wait_send()

        @pl.when(c != chip)
        def _():
            gchip_copy(chip, c).wait_send()
        return 0

    lax.fori_loop(0, nchip, finish, 0)

    def finish_tp(t, _):
        @pl.when(t != mt)
        def _():
            tp_copy(mt, t).wait_send()
        return 0

    lax.fori_loop(0, ntp, finish_tp, 0)


def vmem(n=1):
    specs = [pl.BlockSpec(memory_space=pltpu.VMEM) for _ in range(n)]
    return specs if n > 1 else specs[0]


def shards(hidden, queries, keys_values, w_router, routed, counts, grad_out):
    nseq, ntp = lax.axis_size("seq"), lax.axis_size("tp")
    nchip = nseq // 2
    cap = routed.shape[1]
    tok, width = queries.shape
    heads = width // HEAD_WIDTH
    nq = heads * cap
    scale = 1.0 / math.sqrt(HEAD_WIDTH)
    dma, shape = pltpu.SemaphoreType.DMA, jax.ShapeDtypeStruct
    anywhere = pl.BlockSpec(memory_space=pl.ANY)

    x, q, kvall, logit = pl.pallas_call(
        functools.partial(fetch_kernel, nseq, ntp),
        out_shape=(shape((cap, width), BF16), shape((heads, cap, 128), BF16),
                   shape((nseq, cap, 256), BF16), shape((8, 256), F32)),
        in_specs=[anywhere] * 3 + vmem(2),
        out_specs=tuple(vmem(2)) + (anywhere, vmem()),
        scratch_shapes=[
            pltpu.VMEM((tok, width), BF16), pltpu.VMEM((tok, width), BF16), pltpu.VMEM((2, tok, 128), BF16),
            pltpu.VMEM((cap, 256), BF16), pltpu.VMEM((ntp, 8, 256), F32), dma((4,)), dma((nchip,)), dma((nchip,)), dma((nchip,)),
            dma((nchip,)), dma((ntp,)), dma((ntp,)),
        ],
        compiler_params=pltpu.CompilerParams(
            collective_id=0, has_side_effects=True, vmem_limit_bytes=VMEM_LIMIT),
        name="fetch",
    )(hidden, queries, keys_values, w_router.reshape(1, width), routed)

    live = nseq * cap * LIVE_SHARE[0] // LIVE_SHARE[1]
    span = -(-(live + 15 * nseq) // CHUNK) * CHUNK
    rows = cap + span + CHUNK
    branch, dq, contrib, own, gterm = pl.pallas_call(
        functools.partial(attend_kernel, scale),
        out_shape=(shape((cap, width), BF16), shape((cap, width), BF16),
                   shape((2, nchip, cap, 256), BF16), shape((cap, 256), F32), shape((8, 256), F32)),
        in_specs=[pl.BlockSpec(memory_space=pltpu.SMEM)] + [anywhere] * 3 + [vmem()],
        out_specs=tuple(vmem(2)) + (anywhere,) + tuple(vmem(2)),
        scratch_shapes=[
            pltpu.VMEM((nseq, cap, 256), BF16), pltpu.VMEM((nq, 128), BF16), pltpu.VMEM((cap, width), BF16),
            pltpu.VMEM((2, nchip, cap, 256), BF16), dma((3,)), dma((nseq,)),
            pltpu.VMEM((rows, 256), BF16), pltpu.VMEM((rows, 256), BF16),
            pltpu.VMEM((256, nq), BF16), pltpu.VMEM((256, nq), BF16), pltpu.VMEM((nq, 128), BF16),
            pltpu.VMEM((cap + span, nq), F32), pltpu.VMEM((cap + span, nq), BF16),
            pltpu.VMEM((128, nq), F32), pltpu.VMEM((nq, 128), F32), pltpu.VMEM((rows, 256), BF16),
        ],
        compiler_params=pltpu.CompilerParams(vmem_limit_bytes=VMEM_LIMIT),
        name="attend",
    )(counts, kvall, q.reshape(nq, 128), grad_out, logit)

    dkv, router = pl.pallas_call(
        functools.partial(return_kernel, nseq, ntp),
        out_shape=(shape((2, cap, 128), BF16), shape((8, 128), F32)),
        in_specs=[anywhere, anywhere, vmem(), anywhere],
        out_specs=tuple(vmem(2)),
        scratch_shapes=[
            pltpu.VMEM((nchip, cap, 256), BF16), pltpu.VMEM((cap, 256), F32), pltpu.VMEM((cap, width), BF16), dma((3,)),
            pltpu.VMEM((nchip + 1, cap, 256), BF16), pltpu.VMEM((nchip, cap, 256), BF16),
            pltpu.VMEM((nchip, cap, 256), BF16), pltpu.VMEM((ntp, 8, 256), F32),
            pltpu.VMEM((2, 8, 128), F32), pltpu.VMEM((nchip, 8, 128), F32), pltpu.VMEM((cap, 256), F32),
            dma((nchip,)), dma((nchip,)), dma((nchip,)), dma((nchip,)), dma((ntp,)), dma((ntp,)),
            dma, dma, dma((nchip,)), dma((nchip,)),
        ],
        compiler_params=pltpu.CompilerParams(
            collective_id=1, has_side_effects=True, vmem_limit_bytes=VMEM_LIMIT),
        name="settle",
    )(contrib, own, gterm, x)
    return branch, dq, dkv, router.reshape(8 * 128)


def solution(mesh):
    in_specs = (
        P("seq", "tp"),
        P("seq", "tp"),
        P(None, "seq", "tp"),
        P("tp"),
        P("seq", None),
        P(),
        P("seq", "tp"),
    )
    out_specs = (P("seq", "tp"), P("seq", "tp"), P(None, "seq", "tp"), P("tp"))
    return jax.shard_map(shards, mesh=mesh, in_specs=in_specs, out_specs=out_specs, check_vma=False)
```

```python
import functools
import math

import jax
import jax.numpy as jnp
from jax import lax
from jax.experimental import pallas as pl
from jax.experimental.pallas import tpu as pltpu
from jax.sharding import PartitionSpec as P

HEAD_WIDTH = 128
MESH = pl.DeviceIdType.MESH
NEG = -1e30
VMEM_LIMIT = 62 * 2 ** 20
CHUNK = 256
LIVE_SHARE = (5, 8)
F32 = jnp.float32
BF16 = jnp.bfloat16


def dot_nn(a, b):
    return lax.dot_general(a, b, (((1,), (0,)), ((), ())), preferred_element_type=F32)


def dot_nt(a, b):
    return lax.dot_general(a, b, (((1,), (1,)), ((), ())), preferred_element_type=F32)


def dot_tn(a, b):
    return lax.dot_general(a, b, (((0,), (0,)), ((), ())), preferred_element_type=F32)


def rows_of(row, cap):
    return jnp.broadcast_to(row, (128, cap)).T


class Grid:
    def __init__(self, me, nchip):
        self.side = math.isqrt(nchip)
        self.chip, self.core = me // 2, me % 2
        self.sib = me + 1 - 2 * self.core
        high, low = self.chip // self.side, self.chip % self.side
        self.a = jnp.where(self.core == 0, high, low)
        self.b = jnp.where(self.core == 0, low, high)

    def at(self, a, b):
        return jnp.where(self.core == 0, self.side * a + b, self.side * b + a)

    def device(self, chip):
        return {"seq": 2 * chip + self.core}


def fetch_kernel(nseq, ntp, hid, qry, kv, w, routed, x_out, q_out, kvall, logit_out,
                 hid_v, qry_v, kv_v, held, part, lsem, ssem, ssem2, rsem, fsem, gsem, tssem, trsem):
    me, mt = lax.axis_index("seq"), lax.axis_index("tp")
    nchip = nseq // 2
    chip, core = me // 2, me % 2
    sib = me + 1 - 2 * core
    cap = routed.shape[1]
    tok = hid.shape[0]
    heads = q_out.shape[0]
    load_kv = pltpu.make_async_copy(kv, kv_v, lsem.at[0])
    load_hid = pltpu.make_async_copy(hid, hid_v, lsem.at[1])
    load_qry = pltpu.make_async_copy(qry, qry_v, lsem.at[2])
    load_kv.start()
    load_hid.start()
    load_qry.start()

    barrier = pltpu.get_barrier_semaphore()

    grid = Grid(me, nchip)
    side, last = grid.side, grid.side - 1
    for q in range(side):
        @pl.when(q != grid.b)
        def _():
            pl.semaphore_signal(barrier, inc=1, device_id=grid.device(grid.at(grid.a, q)), device_id_type=MESH)

        @pl.when(q != grid.a)
        def _():
            pl.semaphore_signal(barrier, inc=1, device_id=grid.device(grid.at(q, grid.b)), device_id_type=MESH)

    def greet_tp(t, _):
        @pl.when(t != mt)
        def _():
            pl.semaphore_signal(barrier, inc=1, device_id={"tp": t}, device_id_type=MESH)
        return 0

    pl.semaphore_signal(barrier, inc=1, device_id={"seq": sib}, device_id_type=MESH)
    lax.fori_loop(0, ntp, greet_tp, 0)

    col = rows_of(routed[...].astype(F32), cap)
    lane = lax.broadcasted_iota(jnp.int32, (cap, 128), 1).astype(F32)
    onehot = jnp.concatenate(
        [jnp.where(col == lane + 128.0 * j, 1.0, 0.0).astype(BF16) for j in range(tok // 128)], axis=1
    )
    load_kv.wait()
    held[:, 0:128] = dot_nn(onehot, kv_v[0]).astype(BF16)
    held[:, 128:256] = dot_nn(onehot, kv_v[1]).astype(BF16)
    keep = pltpu.make_async_copy(held, kvall.at[me], lsem.at[3])
    keep.start()

    pl.semaphore_wait(barrier, 2 * last + 1 + ntp - 1)

    def to_line(q):
        return pltpu.make_async_remote_copy(
            src_ref=held, dst_ref=kvall.at[me], send_sem=ssem.at[q], recv_sem=rsem.at[chip],
            device_id=grid.device(grid.at(grid.a, q)), device_id_type=MESH)

    def line_used(q):
        return (q != grid.b) & (chip < grid.at(last, q))

    def own_to_sib():
        return pltpu.make_async_remote_copy(
            src_ref=held, dst_ref=kvall.at[me], send_sem=fsem.at[chip], recv_sem=gsem.at[chip],
            device_id={"seq": sib}, device_id_type=MESH)

    def across(p, q):
        c = grid.at(grid.a, q)
        block = kvall.at[2 * c + core]
        return pltpu.make_async_remote_copy(
            src_ref=block, dst_ref=block, send_sem=ssem2.at[p * side + q], recv_sem=rsem.at[c],
            device_id=grid.device(grid.at(p, grid.b)), device_id_type=MESH)

    def own_across(p):
        return pltpu.make_async_remote_copy(
            src_ref=held, dst_ref=kvall.at[me], send_sem=ssem2.at[p * side + grid.b], recv_sem=rsem.at[chip],
            device_id=grid.device(grid.at(p, grid.b)), device_id_type=MESH)

    def across_used(p, q):
        return (p != grid.a) & (grid.at(grid.a, q) < grid.at(p, grid.b))

    for q in range(side):
        @pl.when(line_used(q))
        def _():
            to_line(q).start()

    for p in range(side):
        @pl.when(across_used(p, grid.b))
        def _():
            own_across(p).start()

    @pl.when(core == 0)
    def _():
        own_to_sib().start()

    def landed(c):
        block = kvall.at[2 * c + core]
        return pltpu.make_async_remote_copy(
            src_ref=block, dst_ref=block, send_sem=fsem.at[c], recv_sem=rsem.at[c],
            device_id={"seq": sib}, device_id_type=MESH)

    def forward(c):
        block = kvall.at[2 * c + core]
        return pltpu.make_async_remote_copy(
            src_ref=block, dst_ref=block, send_sem=fsem.at[c], recv_sem=gsem.at[c],
            device_id={"seq": sib}, device_id_type=MESH)

    def forwarded(c):
        block = kvall.at[2 * c + 1 - core]
        return pltpu.make_async_remote_copy(
            src_ref=block, dst_ref=block, send_sem=fsem.at[c], recv_sem=gsem.at[c],
            device_id={"seq": sib}, device_id_type=MESH)

    load_hid.wait()
    x = dot_nn(onehot, hid_v[...]).astype(BF16)
    x_out[...] = x
    logit = dot_nt(jnp.broadcast_to(w[...], (16, w.shape[1])), x)
    part[mt, :, :] = jnp.zeros((8, 256), F32)
    part[mt, :, 0:cap] = logit[0:8]

    def to_tp(t):
        return pltpu.make_async_remote_copy(
            src_ref=part.at[mt], dst_ref=part.at[mt], send_sem=tssem.at[t], recv_sem=trsem.at[mt],
            device_id={"tp": t}, device_id_type=MESH)

    def from_tp(t):
        return pltpu.make_async_remote_copy(
            src_ref=part.at[t], dst_ref=part.at[t], send_sem=tssem.at[t], recv_sem=trsem.at[t],
            device_id={"tp": t}, device_id_type=MESH)

    def send_tp(t, _):
        @pl.when(t != mt)
        def _():
            to_tp(t).start()
        return 0

    lax.fori_loop(0, ntp, send_tp, 0)

    for q in range(side):
        c = grid.at(grid.a, q)

        @pl.when((q != grid.b) & (c < grid.at(last, grid.b)))
        def _():
            landed(c).wait_recv()

            for p in range(side):
                @pl.when(across_used(p, q))
                def _():
                    across(p, q).start()

            @pl.when(c < chip)
            def _():
                forward(c).start()

    load_qry.wait()
    for h in range(heads):
        q_out[h] = dot_nn(onehot, qry_v[:, h * 128:(h + 1) * 128]).astype(BF16)

    def wait_tp(t, _):
        @pl.when(t != mt)
        def _():
            from_tp(t).wait_recv()
        return 0

    lax.fori_loop(0, ntp, wait_tp, 0)
    total = part[0]
    for t in range(1, ntp):
        total = total + part[t]
    logit_out[...] = total

    for step in range(1, side):
        for q in range(side):
            c = grid.at(lax.rem(grid.a - step + side, side), q)

            @pl.when(c < chip)
            def _():
                landed(c).wait_recv()
                forward(c).start()

    def finish(c, _):
        @pl.when(c < chip)
        def _():
            forwarded(c).wait_recv()
            forward(c).wait_send()
        return 0

    lax.fori_loop(0, nchip, finish, 0)
    for q in range(side):
        @pl.when(line_used(q))
        def _():
            to_line(q).wait_send()

        for p in range(side):
            @pl.when(across_used(p, q))
            def _():
                across(p, q).wait_send()
    keep.wait()

    @pl.when(core == 0)
    def _():
        own_to_sib().wait_send()

    @pl.when(core == 1)
    def _():
        forwarded(chip).wait_recv()

    def finish_tp(t, _):
        @pl.when(t != mt)
        def _():
            to_tp(t).wait_send()
        return 0

    lax.fori_loop(0, ntp, finish_tp, 0)


def attend_kernel(scale, counts, kv_hbm, q_hbm, g_hbm, logit, branch, dq, contrib_hbm, own, gterm,
                  kvall, q, g, contrib, lsem, csem, kx, vx, qtx, dotx, dob, s_scr, e_scr, ot, wide, dkv):
    me = lax.axis_index("seq")
    cap, width = g.shape
    nq = q.shape[0]
    heads = width // 128
    to_exp2 = scale * math.log2(math.e)
    live_here = counts[me]
    loads = [
        pltpu.make_async_copy(kv_hbm.at[me], kvall.at[me], lsem.at[0]),
        pltpu.make_async_copy(q_hbm, q, lsem.at[1]),
        pltpu.make_async_copy(g_hbm, g, lsem.at[2]),
    ]
    for load in loads:
        load.start()

    def block_load(s):
        return pltpu.make_async_copy(kv_hbm.at[s], kvall.at[s], csem.at[s])

    def start_load(s, _):
        block_load(s).start()
        return 0

    lax.fori_loop(0, me, start_load, 0)

    row = lax.broadcasted_iota(jnp.int32, (cap, 128), 0)
    lane = lax.broadcasted_iota(jnp.int32, (cap, 128), 1)
    ones3 = jnp.where(lane < 3, 1.0, 0.0).astype(BF16)
    loads[0].wait()
    kx[0:cap, 0:128] = kvall[me, :, 0:128]
    kx[0:cap, 128:256] = jnp.zeros((cap, 128), BF16)
    vx[0:cap, 0:128] = kvall[me, :, 128:256]
    vx[0:cap, 128:256] = ones3

    def place(s, off):
        block_load(s).wait()
        off = pl.multiple_of(off, 16)
        n = counts[s]
        kx[pl.ds(off, cap), 0:128] = kvall[s, :, 0:128]
        kx[pl.ds(off, cap), 128:256] = jnp.where((row >= n) & (lane == 0), NEG, 0.0).astype(BF16)
        vx[pl.ds(off, cap), 0:128] = kvall[s, :, 128:256]
        vx[pl.ds(off, cap), 128:256] = ones3
        return off + ((n + 15) // 16) * 16

    end = pl.multiple_of(lax.fori_loop(0, me, place, cap), 16)
    kx[pl.ds(end, CHUNK), 0:128] = jnp.zeros((CHUNK, 128), BF16)
    kx[pl.ds(end, CHUNK), 128:256] = jnp.where(
        lax.broadcasted_iota(jnp.int32, (CHUNK, 128), 1) == 0, NEG, 0.0).astype(BF16)
    vx[pl.ds(end, CHUNK), :] = jnp.zeros((CHUNK, 256), BF16)
    chunks = (end - cap + CHUNK - 1) // CHUNK
    doubles = chunks // 2

    def at(c, size):
        return pl.ds(pl.multiple_of(cap + c * CHUNK, 32), size * CHUNK)

    def sweep(step, carry):
        carry = lax.fori_loop(0, doubles, lambda c, held: step(at(2 * c, 2), 2 * CHUNK, held), carry)
        return lax.fori_loop(2 * doubles, chunks, lambda c, held: step(at(c, 1), CHUNK, held), carry)

    loads[1].wait()

    qtx[0:128, :] = q[...].T
    first = lax.broadcasted_iota(jnp.int32, (128, nq), 0)
    qtx[128:256, :] = jnp.where(first == 0, 1.0, 0.0).astype(BF16)

    key_slot = lax.broadcasted_iota(jnp.int32, (cap, nq), 0)
    pos = lax.broadcasted_iota(jnp.int32, (cap, nq), 1)
    query_slot = pos
    for h in range(1, heads):
        query_slot = query_slot - jnp.where(pos >= h * cap, cap, 0)
    s = jnp.where(key_slot <= query_slot, dot_nn(kx[0:cap, :], qtx[...]), NEG)
    s_scr[0:cap, :] = s
    top = jnp.max(s.reshape(cap // 8, 8, nq), axis=0)

    def score(sl, rows, top):
        s = dot_nn(kx[sl, :], qtx[...])
        s_scr[sl, :] = s
        return jnp.maximum(top, jnp.max(s.reshape(rows // 8, 8, nq), axis=0))

    top = sweep(score, top)
    top = jnp.max(top, axis=0, keepdims=True) * to_exp2

    def soften(sl, rows, total, start):
        e = jnp.exp2(s_scr[sl, :] * to_exp2 - top)
        eb = e.astype(BF16)
        e_scr[sl, :] = eb
        add = dot_tn(vx[sl, 0:128], eb)
        ot[...] = add if start else ot[...] + add
        return total + jnp.sum(e.reshape(rows // 8, 8, nq), axis=0)

    total = soften(pl.ds(0, cap), cap, jnp.zeros((8, nq), F32), True)
    total = sweep(lambda sl, rows, t: soften(sl, rows, t, False), total)
    inverse = 1.0 / jnp.sum(total, axis=0, keepdims=True)

    z = logit[0:1, 0:cap]
    gate = 1.0 / (1.0 + jnp.exp(-z))
    live = lax.broadcasted_iota(jnp.int32, (1, cap), 1) < live_here
    weight = rows_of(jnp.where(live, gate, 0.0), cap)
    factor = jnp.where(live, gate * (1.0 - gate), 0.0)
    ot[...] = ot[...] * inverse
    wide[...] = ot[...].T
    loads[2].wait()
    acc = jnp.zeros((cap, 128), F32)
    for h in range(heads):
        rows, lanes = slice(h * cap, (h + 1) * cap), slice(h * 128, (h + 1) * 128)
        o = wide[rows, :]
        up = g[:, lanes].astype(F32)
        branch[:, lanes] = (o * weight).astype(BF16)
        acc = acc + up * o
        wide[rows, :] = up * weight
    gterm[0:8, :] = jnp.zeros((8, 256), F32)
    gterm[0:1, 0:cap] = jnp.sum(acc.T, axis=0, keepdims=True)
    gterm[1:2, 0:cap] = factor
    cot = (wide[...].T * inverse).astype(BF16)
    dotx[0:128, :] = cot
    cotf = cot.astype(F32)
    delta = -jnp.sum(cotf * ot[...], axis=0, keepdims=True)
    d1 = delta.astype(BF16).astype(F32)
    d2 = (delta - d1).astype(BF16).astype(F32)
    d3 = delta - d1 - d2
    dotx[128:256, :] = jnp.where(
        first == 0, d1, jnp.where(first == 1, d2, jnp.where(first == 2, d3, 0.0))).astype(BF16)
    dob[...] = cotf.T.astype(BF16)

    def back(sl, start):
        e = e_scr[sl, :]
        ds = e * dot_nn(vx[sl, :], dotx[...]).astype(BF16)
        add = dot_tn(kx[sl, 0:128], ds)
        wide_t = ot
        wide_t[...] = add if start else wide_t[...] + add
        return dot_nn(ds, q[...]) * scale, dot_nn(e, dob[...])

    dk, dv = back(pl.ds(0, cap), True)
    own[:, 0:128] = dk
    own[:, 128:256] = dv

    def back_chunk(sl, rows, _):
        dk, dv = back(sl, False)
        dkv[sl, 0:128] = dk.astype(BF16)
        dkv[sl, 128:256] = dv.astype(BF16)
        return 0

    sweep(back_chunk, 0)
    row2 = lax.broadcasted_iota(jnp.int32, (cap, 256), 0)

    def block_store(s):
        return pltpu.make_async_copy(contrib.at[s % 2, s // 2], contrib_hbm.at[s % 2, s // 2], csem.at[s])

    def unplace(s, off):
        off = pl.multiple_of(off, 16)
        n = counts[s]
        block = dkv[pl.ds(off, cap), :].astype(F32)
        contrib[s % 2, s // 2] = jnp.where(row2 < n, block, 0.0).astype(BF16)
        block_store(s).start()
        return off + ((n + 15) // 16) * 16

    lax.fori_loop(0, me, unplace, cap)

    wide[...] = (ot[...] * scale).T
    for h in range(heads):
        dq[:, h * 128:(h + 1) * 128] = wide[h * cap:(h + 1) * cap, :].astype(BF16)

    def finish_store(s, _):
        block_store(s).wait()
        return 0

    lax.fori_loop(0, me, finish_store, 0)


def return_kernel(nseq, ntp, contrib, own_hbm, gterm, x_hbm, dkv_out, router_out,
                  half, own, x, lsem, pair, mine, inbox, inbox2, turn, part, gpair, gchip, sums, psem, prsem, ssem, rsem, s2sem, r2sem, tssem, trsem,
                  qsem, qrsem, gssem, grsem):
    me, mt = lax.axis_index("seq"), lax.axis_index("tp")
    nchip = nseq // 2
    chip, core = me // 2, me % 2
    sib = me + 1 - 2 * core
    cap = x.shape[0]
    loads = [
        pltpu.make_async_copy(contrib.at[core], half, lsem.at[0]),
        pltpu.make_async_copy(own_hbm, own, lsem.at[1]),
        pltpu.make_async_copy(x_hbm, x, lsem.at[2]),
    ]
    for load in loads:
        load.start()

    barrier = pltpu.get_barrier_semaphore()

    def greet_chip(c, _):
        @pl.when(c != chip)
        def _():
            pl.semaphore_signal(barrier, inc=1, device_id={"seq": 2 * c + core}, device_id_type=MESH)
        return 0

    def greet_tp(t, _):
        @pl.when(t != mt)
        def _():
            pl.semaphore_signal(barrier, inc=1, device_id={"tp": t}, device_id_type=MESH)
        return 0

    lax.fori_loop(0, nchip, greet_chip, 0)
    pl.semaphore_signal(barrier, inc=1, device_id={"seq": sib}, device_id_type=MESH)
    lax.fori_loop(0, ntp, greet_tp, 0)
    part[mt] = gterm[...]
    pl.semaphore_wait(barrier, nchip - 1 + 1 + ntp - 1)

    def tp_copy(slot, t):
        return pltpu.make_async_remote_copy(
            src_ref=part.at[slot], dst_ref=part.at[slot], send_sem=tssem.at[t], recv_sem=trsem.at[slot],
            device_id={"tp": t}, device_id_type=MESH)

    def send_tp(t, _):
        @pl.when(t != mt)
        def _():
            tp_copy(mt, t).start()
        return 0

    lax.fori_loop(0, ntp, send_tp, 0)

    def pair_copy(c):
        return pltpu.make_async_remote_copy(
            src_ref=contrib.at[1 - core, c], dst_ref=pair.at[c], send_sem=psem.at[c], recv_sem=prsem.at[c],
            device_id={"seq": sib}, device_id_type=MESH)

    def send_pair(c, _):
        @pl.when((c < chip) | ((c == chip) & (core == 1)))
        def _():
            pair_copy(c).start()
        return 0

    lax.fori_loop(0, nchip, send_pair, 0)

    grid = Grid(me, nchip)
    side, last = grid.side, grid.side - 1

    def first_copy(p, q):
        return pltpu.make_async_remote_copy(
            src_ref=mine.at[grid.at(p, q)], dst_ref=inbox.at[grid.a, q], send_sem=ssem.at[p * side + q],
            recv_sem=rsem.at[grid.a * side + q], device_id=grid.device(grid.at(p, grid.b)), device_id_type=MESH)

    def first_landed(p, q):
        return pltpu.make_async_remote_copy(
            src_ref=inbox.at[p, q], dst_ref=inbox.at[p, q], send_sem=ssem.at[p * side + q],
            recv_sem=rsem.at[p * side + q], device_id=grid.device(grid.at(p, grid.b)), device_id_type=MESH)

    def second_copy(q):
        return pltpu.make_async_remote_copy(
            src_ref=turn.at[q], dst_ref=inbox2.at[grid.b], send_sem=s2sem.at[q], recv_sem=r2sem.at[grid.b],
            device_id=grid.device(grid.at(grid.a, q)), device_id_type=MESH)

    def second_landed(q):
        return pltpu.make_async_remote_copy(
            src_ref=inbox2.at[q], dst_ref=inbox2.at[q], send_sem=s2sem.at[q], recv_sem=r2sem.at[q],
            device_id=grid.device(grid.at(grid.a, q)), device_id_type=MESH)

    loads[0].wait()

    def join(c):
        pair_copy(c).wait_recv()
        mine[c] = (half[c].astype(F32) + pair[c].astype(F32)).astype(BF16)

    for p in range(side):
        for q in range(side):
            @pl.when((p != grid.a) & (grid.at(p, q) < chip))
            def _():
                join(grid.at(p, q))
                first_copy(p, q).start()

    for q in range(side):
        @pl.when(grid.at(grid.a, q) < chip)
        def _():
            join(grid.at(grid.a, q))

    def wait_tp(t, _):
        @pl.when(t != mt)
        def _():
            tp_copy(t, t).wait_recv()
        return 0

    lax.fori_loop(0, ntp, wait_tp, 0)
    total = part[0, 0:1, :]
    for t in range(1, ntp):
        total = total + part[t, 0:1, :]
    dlogit = (total * gterm[1:2, :])[:, 0:cap]
    p1 = dlogit.astype(BF16)
    r1 = dlogit - p1.astype(F32)
    p2 = r1.astype(BF16)
    p3 = (r1 - p2.astype(F32)).astype(BF16)
    loads[2].wait()
    xs = x[...]
    share = (dot_nn(jnp.broadcast_to(p1, (16, cap)), xs) + dot_nn(jnp.broadcast_to(p2, (16, cap)), xs)
             + dot_nn(jnp.broadcast_to(p3, (16, cap)), xs))
    for i in range(x.shape[1] // 128):
        gpair[core, i:i + 1, :] = share[0:1, i * 128:(i + 1) * 128]

    def gpair_copy(slot):
        return pltpu.make_async_remote_copy(
            src_ref=gpair.at[slot], dst_ref=gpair.at[slot], send_sem=qsem, recv_sem=qrsem,
            device_id={"seq": sib}, device_id_type=MESH)

    gpair_copy(core).start()
    gpair_copy(1 - core).wait_recv()
    gchip[chip] = gpair[0] + gpair[1]

    def gchip_copy(slot, c):
        return pltpu.make_async_remote_copy(
            src_ref=gchip.at[slot], dst_ref=gchip.at[slot], send_sem=gssem.at[c], recv_sem=grsem.at[slot],
            device_id={"seq": 2 * c + core}, device_id_type=MESH)

    def send_gchip(c, _):
        @pl.when(c != chip)
        def _():
            gchip_copy(chip, c).start()
        return 0

    lax.fori_loop(0, nchip, send_gchip, 0)

    for q in range(side):
        target = grid.at(grid.a, q)

        @pl.when((q != grid.b) & (target < grid.at(last, grid.b)))
        def _():
            @pl.when(target < chip)
            def _():
                sums[...] = mine[target].astype(F32)

            @pl.when(target >= chip)
            def _():
                sums[...] = jnp.zeros((cap, 256), F32)

            for p in range(side):
                @pl.when((p != grid.a) & (target < grid.at(p, grid.b)))
                def _():
                    first_landed(p, q).wait_recv()
                    sums[...] = sums[...] + inbox[p, q].astype(F32)
            turn[q] = sums[...].astype(BF16)
            second_copy(q).start()

    @pl.when(core == 0)
    def _():
        pair_copy(chip).wait_recv()
        pair[nchip] = pair[chip]

    @pl.when(core == 1)
    def _():
        pair[nchip] = jnp.zeros((cap, 256), BF16)

    loads[1].wait()
    sums[...] = own[...] + pair[nchip].astype(F32)

    for p in range(side):
        @pl.when((p != grid.a) & (chip < grid.at(p, grid.b)))
        def _():
            first_landed(p, grid.b).wait_recv()
            sums[...] = sums[...] + inbox[p, grid.b].astype(F32)

    for q in range(side):
        @pl.when((q != grid.b) & (chip < grid.at(last, q)))
        def _():
            second_landed(q).wait_recv()
            sums[...] = sums[...] + inbox2[q].astype(F32)
    dkv_out[0] = sums[:, 0:128].astype(BF16)
    dkv_out[1] = sums[:, 128:256].astype(BF16)

    def wait_gchip(c, _):
        @pl.when(c != chip)
        def _():
            gchip_copy(c, c).wait_recv()
        return 0

    lax.fori_loop(0, nchip, wait_gchip, 0)
    total = gchip[0]
    for c in range(1, nchip):
        total = total + gchip[c]
    router_out[...] = total

    gpair_copy(core).wait_send()

    def finish(c, _):
        @pl.when((c < chip) | ((c == chip) & (core == 1)))
        def _():
            pair_copy(c).wait_send()

        @pl.when(c != chip)
        def _():
            gchip_copy(chip, c).wait_send()
        return 0

    lax.fori_loop(0, nchip, finish, 0)

    for q in range(side):
        for p in range(side):
            @pl.when((p != grid.a) & (grid.at(p, q) < chip))
            def _():
                first_copy(p, q).wait_send()

        @pl.when((q != grid.b) & (grid.at(grid.a, q) < grid.at(last, grid.b)))
        def _():
            second_copy(q).wait_send()

    def finish_tp(t, _):
        @pl.when(t != mt)
        def _():
            tp_copy(mt, t).wait_send()
        return 0

    lax.fori_loop(0, ntp, finish_tp, 0)


def vmem(n=1):
    specs = [pl.BlockSpec(memory_space=pltpu.VMEM) for _ in range(n)]
    return specs if n > 1 else specs[0]


def shards(hidden, queries, keys_values, w_router, routed, counts, grad_out):
    nseq, ntp = lax.axis_size("seq"), lax.axis_size("tp")
    nchip = nseq // 2
    side = math.isqrt(nchip)
    cap = routed.shape[1]
    tok, width = queries.shape
    heads = width // HEAD_WIDTH
    nq = heads * cap
    scale = 1.0 / math.sqrt(HEAD_WIDTH)
    dma, shape = pltpu.SemaphoreType.DMA, jax.ShapeDtypeStruct
    anywhere = pl.BlockSpec(memory_space=pl.ANY)

    x, q, kvall, logit = pl.pallas_call(
        functools.partial(fetch_kernel, nseq, ntp),
        out_shape=(shape((cap, width), BF16), shape((heads, cap, 128), BF16),
                   shape((nseq, cap, 256), BF16), shape((8, 256), F32)),
        in_specs=[anywhere] * 3 + vmem(2),
        out_specs=tuple(vmem(2)) + (anywhere, vmem()),
        scratch_shapes=[
            pltpu.VMEM((tok, width), BF16), pltpu.VMEM((tok, width), BF16), pltpu.VMEM((2, tok, 128), BF16),
            pltpu.VMEM((cap, 256), BF16), pltpu.VMEM((ntp, 8, 256), F32), dma((4,)), dma((nchip,)), dma((nchip,)), dma((nchip,)), dma((nchip,)),
            dma((nchip,)), dma((ntp,)), dma((ntp,)),
        ],
        compiler_params=pltpu.CompilerParams(
            collective_id=0, has_side_effects=True, vmem_limit_bytes=VMEM_LIMIT),
        name="fetch",
    )(hidden, queries, keys_values, w_router.reshape(1, width), routed)

    live = nseq * cap * LIVE_SHARE[0] // LIVE_SHARE[1]
    span = -(-(live + 15 * nseq) // CHUNK) * CHUNK
    rows = cap + span + CHUNK
    branch, dq, contrib, own, gterm = pl.pallas_call(
        functools.partial(attend_kernel, scale),
        out_shape=(shape((cap, width), BF16), shape((cap, width), BF16),
                   shape((2, nchip, cap, 256), BF16), shape((cap, 256), F32), shape((8, 256), F32)),
        in_specs=[pl.BlockSpec(memory_space=pltpu.SMEM)] + [anywhere] * 3 + [vmem()],
        out_specs=tuple(vmem(2)) + (anywhere,) + tuple(vmem(2)),
        scratch_shapes=[
            pltpu.VMEM((nseq, cap, 256), BF16), pltpu.VMEM((nq, 128), BF16), pltpu.VMEM((cap, width), BF16),
            pltpu.VMEM((2, nchip, cap, 256), BF16), dma((3,)), dma((nseq,)),
            pltpu.VMEM((rows, 256), BF16), pltpu.VMEM((rows, 256), BF16),
            pltpu.VMEM((256, nq), BF16), pltpu.VMEM((256, nq), BF16), pltpu.VMEM((nq, 128), BF16),
            pltpu.VMEM((cap + span, nq), F32), pltpu.VMEM((cap + span, nq), BF16),
            pltpu.VMEM((128, nq), F32), pltpu.VMEM((nq, 128), F32), pltpu.VMEM((rows, 256), BF16),
        ],
        compiler_params=pltpu.CompilerParams(vmem_limit_bytes=VMEM_LIMIT),
        name="attend",
    )(counts, kvall, q.reshape(nq, 128), grad_out, logit)

    dkv, router = pl.pallas_call(
        functools.partial(return_kernel, nseq, ntp),
        out_shape=(shape((2, cap, 128), BF16), shape((width // 128, 128), F32)),
        in_specs=[anywhere, anywhere, vmem(), anywhere],
        out_specs=tuple(vmem(2)),
        scratch_shapes=[
            pltpu.VMEM((nchip, cap, 256), BF16), pltpu.VMEM((cap, 256), F32), pltpu.VMEM((cap, width), BF16), dma((3,)),
            pltpu.VMEM((nchip + 1, cap, 256), BF16), pltpu.VMEM((nchip, cap, 256), BF16),
            pltpu.VMEM((side, side, cap, 256), BF16), pltpu.VMEM((side, cap, 256), BF16),
            pltpu.VMEM((side, cap, 256), BF16), pltpu.VMEM((ntp, 8, 256), F32),
            pltpu.VMEM((2, width // 128, 128), F32), pltpu.VMEM((nchip, width // 128, 128), F32), pltpu.VMEM((cap, 256), F32),
            dma((nchip,)), dma((nchip,)), dma((nchip,)), dma((nchip,)), dma((side,)), dma((side,)), dma((ntp,)), dma((ntp,)),
            dma, dma, dma((nchip,)), dma((nchip,)),
        ],
        compiler_params=pltpu.CompilerParams(
            collective_id=1, has_side_effects=True, vmem_limit_bytes=VMEM_LIMIT),
        name="settle",
    )(contrib, own, gterm, x)
    return branch, dq, dkv, router.reshape(width)


def solution(mesh):
    in_specs = (
        P("seq", "tp"),
        P("seq", "tp"),
        P(None, "seq", "tp"),
        P("tp"),
        P("seq", None),
        P(),
        P("seq", "tp"),
    )
    out_specs = (P("seq", "tp"), P("seq", "tp"), P(None, "seq", "tp"), P("tp"))
    return jax.shard_map(shards, mesh=mesh, in_specs=in_specs, out_specs=out_specs, check_vma=False)
```

```python
import functools
import math

import jax
import jax.numpy as jnp
from jax import lax
from jax.experimental import pallas as pl
from jax.experimental.pallas import tpu as pltpu
from jax.sharding import PartitionSpec as P

HEAD_WIDTH = 128
MESH = pl.DeviceIdType.MESH
NEG = -1e30
VMEM_LIMIT = 62 * 2 ** 20
CHUNK = 256
LIVE_SHARE = (5, 8)
F32 = jnp.float32
BF16 = jnp.bfloat16


def dot_nn(a, b):
    return lax.dot_general(a, b, (((1,), (0,)), ((), ())), preferred_element_type=F32)


def dot_nt(a, b):
    return lax.dot_general(a, b, (((1,), (1,)), ((), ())), preferred_element_type=F32)


def dot_tn(a, b):
    return lax.dot_general(a, b, (((0,), (0,)), ((), ())), preferred_element_type=F32)


def rows_of(row, cap):
    return jnp.broadcast_to(row, (128, cap)).T


class Grid:
    def __init__(self, me, nchip):
        self.side = math.isqrt(nchip)
        self.chip, self.core = me // 2, me % 2
        self.sib = me + 1 - 2 * self.core
        high, low = self.chip // self.side, self.chip % self.side
        self.a = jnp.where(self.core == 0, high, low)
        self.b = jnp.where(self.core == 0, low, high)

    def at(self, a, b):
        return jnp.where(self.core == 0, self.side * a + b, self.side * b + a)

    def device(self, chip):
        return {"seq": 2 * chip + self.core}


def fetch_kernel(nseq, ntp, hid, qry, kv, w, routed, x_out, q_out, kvall, logit_out,
                 hid_v, qry_v, kv_v, held, part, lsem, ssem, ssem2, rsem, fsem, gsem, tssem, trsem):
    me, mt = lax.axis_index("seq"), lax.axis_index("tp")
    nchip = nseq // 2
    chip, core = me // 2, me % 2
    sib = me + 1 - 2 * core
    cap = routed.shape[1]
    tok = hid.shape[0]
    heads = q_out.shape[0]
    load_kv = pltpu.make_async_copy(kv, kv_v, lsem.at[0])
    load_hid = pltpu.make_async_copy(hid, hid_v, lsem.at[1])
    load_qry = pltpu.make_async_copy(qry, qry_v, lsem.at[2])
    load_kv.start()
    load_hid.start()
    load_qry.start()

    barrier = pltpu.get_barrier_semaphore()

    grid = Grid(me, nchip)
    side, last = grid.side, grid.side - 1
    for q in range(side):
        @pl.when(q != grid.b)
        def _():
            pl.semaphore_signal(barrier, inc=1, device_id=grid.device(grid.at(grid.a, q)), device_id_type=MESH)

        @pl.when(q != grid.a)
        def _():
            pl.semaphore_signal(barrier, inc=1, device_id=grid.device(grid.at(q, grid.b)), device_id_type=MESH)

    def greet_tp(t, _):
        @pl.when(t != mt)
        def _():
            pl.semaphore_signal(barrier, inc=1, device_id={"tp": t}, device_id_type=MESH)
        return 0

    pl.semaphore_signal(barrier, inc=1, device_id={"seq": sib}, device_id_type=MESH)
    lax.fori_loop(0, ntp, greet_tp, 0)

    col = rows_of(routed[...].astype(F32), cap)
    lane = lax.broadcasted_iota(jnp.int32, (cap, 128), 1).astype(F32)
    onehot = jnp.concatenate(
        [jnp.where(col == lane + 128.0 * j, 1.0, 0.0).astype(BF16) for j in range(tok // 128)], axis=1
    )
    load_kv.wait()
    held[:, 0:128] = dot_nn(onehot, kv_v[0]).astype(BF16)
    held[:, 128:256] = dot_nn(onehot, kv_v[1]).astype(BF16)
    keep = pltpu.make_async_copy(held, kvall.at[me], lsem.at[3])
    keep.start()

    pl.semaphore_wait(barrier, 2 * last + 1 + ntp - 1)

    def to_line(q):
        return pltpu.make_async_remote_copy(
            src_ref=held, dst_ref=kvall.at[me], send_sem=ssem.at[q], recv_sem=rsem.at[chip],
            device_id=grid.device(grid.at(grid.a, q)), device_id_type=MESH)

    def line_used(q):
        return (q != grid.b) & (chip < grid.at(last, q))

    def own_to_sib():
        return pltpu.make_async_remote_copy(
            src_ref=held, dst_ref=kvall.at[me], send_sem=fsem.at[chip], recv_sem=gsem.at[chip],
            device_id={"seq": sib}, device_id_type=MESH)

    def across(p, q):
        c = grid.at(grid.a, q)
        block = kvall.at[2 * c + core]
        return pltpu.make_async_remote_copy(
            src_ref=block, dst_ref=block, send_sem=ssem2.at[p * side + q], recv_sem=rsem.at[c],
            device_id=grid.device(grid.at(p, grid.b)), device_id_type=MESH)

    def own_across(p):
        return pltpu.make_async_remote_copy(
            src_ref=held, dst_ref=kvall.at[me], send_sem=ssem2.at[p * side + grid.b], recv_sem=rsem.at[chip],
            device_id=grid.device(grid.at(p, grid.b)), device_id_type=MESH)

    def across_used(p, q):
        return (p != grid.a) & (grid.at(grid.a, q) < grid.at(p, grid.b))

    for q in range(side):
        @pl.when(line_used(q))
        def _():
            to_line(q).start()

    for p in range(side):
        @pl.when(across_used(p, grid.b))
        def _():
            own_across(p).start()

    @pl.when(core == 0)
    def _():
        own_to_sib().start()

    def landed(c):
        block = kvall.at[2 * c + core]
        return pltpu.make_async_remote_copy(
            src_ref=block, dst_ref=block, send_sem=fsem.at[c], recv_sem=rsem.at[c],
            device_id={"seq": sib}, device_id_type=MESH)

    def forward(c):
        block = kvall.at[2 * c + core]
        return pltpu.make_async_remote_copy(
            src_ref=block, dst_ref=block, send_sem=fsem.at[c], recv_sem=gsem.at[c],
            device_id={"seq": sib}, device_id_type=MESH)

    def forwarded(c):
        block = kvall.at[2 * c + 1 - core]
        return pltpu.make_async_remote_copy(
            src_ref=block, dst_ref=block, send_sem=fsem.at[c], recv_sem=gsem.at[c],
            device_id={"seq": sib}, device_id_type=MESH)

    load_hid.wait()
    x = dot_nn(onehot, hid_v[...]).astype(BF16)
    x_out[...] = x
    logit = dot_nt(jnp.broadcast_to(w[...].reshape(1, w.shape[0]), (16, w.shape[0])), x)
    part[mt, :, :] = jnp.zeros((8, 256), F32)
    part[mt, :, 0:cap] = logit[0:8]

    def to_tp(t):
        return pltpu.make_async_remote_copy(
            src_ref=part.at[mt], dst_ref=part.at[mt], send_sem=tssem.at[t], recv_sem=trsem.at[mt],
            device_id={"tp": t}, device_id_type=MESH)

    def from_tp(t):
        return pltpu.make_async_remote_copy(
            src_ref=part.at[t], dst_ref=part.at[t], send_sem=tssem.at[t], recv_sem=trsem.at[t],
            device_id={"tp": t}, device_id_type=MESH)

    def send_tp(t, _):
        @pl.when(t != mt)
        def _():
            to_tp(t).start()
        return 0

    lax.fori_loop(0, ntp, send_tp, 0)

    for q in range(side):
        c = grid.at(grid.a, q)

        @pl.when((q != grid.b) & (c < grid.at(last, grid.b)))
        def _():
            landed(c).wait_recv()

            for p in range(side):
                @pl.when(across_used(p, q))
                def _():
                    across(p, q).start()

            @pl.when(c < chip)
            def _():
                forward(c).start()

    load_qry.wait()
    for h in range(heads):
        q_out[h] = dot_nn(onehot, qry_v[:, h * 128:(h + 1) * 128]).astype(BF16)

    def wait_tp(t, _):
        @pl.when(t != mt)
        def _():
            from_tp(t).wait_recv()
        return 0

    lax.fori_loop(0, ntp, wait_tp, 0)
    total = part[0]
    for t in range(1, ntp):
        total = total + part[t]
    logit_out[...] = total

    for step in range(1, side):
        for q in range(side):
            c = grid.at(lax.rem(grid.a - step + side, side), q)

            @pl.when(c < chip)
            def _():
                landed(c).wait_recv()
                forward(c).start()

    for q in range(side):
        @pl.when(line_used(q))
        def _():
            to_line(q).wait_send()

    keep.wait()

    @pl.when(core == 0)
    def _():
        own_to_sib().wait_send()

    def finish_tp(t, _):
        @pl.when(t != mt)
        def _():
            to_tp(t).wait_send()
        return 0

    lax.fori_loop(0, ntp, finish_tp, 0)
    for q in range(side):
        for p in range(side):
            @pl.when(across_used(p, q))
            def _():
                across(p, q).wait_send()

    def finish_send(c, _):
        @pl.when(c < chip)
        def _():
            forward(c).wait_send()
        return 0

    def finish(c, _):
        @pl.when(c < chip)
        def _():
            forwarded(c).wait_recv()
        return 0

    lax.fori_loop(0, nchip, finish_send, 0)

    @pl.when(core == 1)
    def _():
        forwarded(chip).wait_recv()

    lax.fori_loop(0, nchip, finish, 0)


def attend_kernel(scale, counts, kv_hbm, q_hbm, g_hbm, logit, branch, dq, contrib_hbm, own, gterm,
                  kvall, q, g, contrib, lsem, csem, kx, vx, qtx, dotx, dob, s_scr, e_scr, ot, wide, dkv):
    me = lax.axis_index("seq")
    cap, width = g.shape
    nq = q.shape[0]
    heads = width // 128
    to_exp2 = scale * math.log2(math.e)
    live_here = counts[me]
    loads = [
        pltpu.make_async_copy(kv_hbm.at[me], kvall.at[me], lsem.at[0]),
        pltpu.make_async_copy(q_hbm, q, lsem.at[1]),
        pltpu.make_async_copy(g_hbm, g, lsem.at[2]),
    ]
    for load in loads:
        load.start()

    def block_load(s):
        return pltpu.make_async_copy(kv_hbm.at[s], kvall.at[s], csem.at[s])

    def start_load(s, _):
        block_load(s).start()
        return 0

    lax.fori_loop(0, me, start_load, 0)

    row = lax.broadcasted_iota(jnp.int32, (cap, 128), 0)
    lane = lax.broadcasted_iota(jnp.int32, (cap, 128), 1)
    ones3 = jnp.where(lane < 3, 1.0, 0.0).astype(BF16)
    loads[0].wait()
    kx[0:cap, 0:128] = kvall[me, :, 0:128]
    kx[0:cap, 128:256] = jnp.zeros((cap, 128), BF16)
    vx[0:cap, 0:128] = kvall[me, :, 128:256]
    vx[0:cap, 128:256] = ones3

    def place(s, off):
        block_load(s).wait()
        off = pl.multiple_of(off, 16)
        n = counts[s]
        kx[pl.ds(off, cap), 0:128] = kvall[s, :, 0:128]
        kx[pl.ds(off, cap), 128:256] = jnp.where((row >= n) & (lane == 0), NEG, 0.0).astype(BF16)
        vx[pl.ds(off, cap), 0:128] = kvall[s, :, 128:256]
        vx[pl.ds(off, cap), 128:256] = ones3
        return off + ((n + 15) // 16) * 16

    end = pl.multiple_of(lax.fori_loop(0, me, place, cap), 16)
    kx[pl.ds(end, CHUNK), 0:128] = jnp.zeros((CHUNK, 128), BF16)
    kx[pl.ds(end, CHUNK), 128:256] = jnp.where(
        lax.broadcasted_iota(jnp.int32, (CHUNK, 128), 1) == 0, NEG, 0.0).astype(BF16)
    vx[pl.ds(end, CHUNK), :] = jnp.zeros((CHUNK, 256), BF16)
    chunks = (end - cap + CHUNK - 1) // CHUNK
    doubles = chunks // 2

    def at(c, size):
        return pl.ds(pl.multiple_of(cap + c * CHUNK, 32), size * CHUNK)

    def sweep(step, carry):
        quads = chunks // 4
        carry = lax.fori_loop(0, quads, lambda c, held: step(at(4 * c, 4), 4 * CHUNK, held), carry)
        carry = lax.fori_loop(
            2 * quads, doubles, lambda c, held: step(at(2 * c, 2), 2 * CHUNK, held), carry)
        return lax.fori_loop(2 * doubles, chunks, lambda c, held: step(at(c, 1), CHUNK, held), carry)

    loads[1].wait()

    qtx[0:128, :] = q[...].T
    first = lax.broadcasted_iota(jnp.int32, (128, nq), 0)
    qtx[128:256, :] = jnp.where(first == 0, 1.0, 0.0).astype(BF16)

    key_slot = lax.broadcasted_iota(jnp.int32, (cap, nq), 0)
    pos = lax.broadcasted_iota(jnp.int32, (cap, nq), 1)
    query_slot = pos
    for h in range(1, heads):
        query_slot = query_slot - jnp.where(pos >= h * cap, cap, 0)
    s = jnp.where(key_slot <= query_slot, dot_nn(kx[0:cap, :], qtx[...]), NEG)
    s_scr[0:cap, :] = s
    top = jnp.max(s.reshape(cap // 8, 8, nq), axis=0)

    def score(sl, rows, top):
        s = dot_nn(kx[sl, :], qtx[...])
        s_scr[sl, :] = s
        return jnp.maximum(top, jnp.max(s.reshape(rows // 8, 8, nq), axis=0))

    top = sweep(score, top)
    top = jnp.max(top, axis=0, keepdims=True) * to_exp2

    def soften(sl, rows, total, start):
        e = jnp.exp2(s_scr[sl, :] * to_exp2 - top)
        eb = e.astype(BF16)
        e_scr[sl, :] = eb
        add = dot_tn(vx[sl, 0:128], eb)
        ot[...] = add if start else ot[...] + add
        return total + jnp.sum(e.reshape(rows // 8, 8, nq), axis=0)

    total = soften(pl.ds(0, cap), cap, jnp.zeros((8, nq), F32), True)
    total = sweep(lambda sl, rows, t: soften(sl, rows, t, False), total)
    inverse = 1.0 / jnp.sum(total, axis=0, keepdims=True)

    z = logit[0:1, 0:cap]
    gate = 1.0 / (1.0 + jnp.exp(-z))
    live = lax.broadcasted_iota(jnp.int32, (1, cap), 1) < live_here
    weight = rows_of(jnp.where(live, gate, 0.0), cap)
    factor = jnp.where(live, gate * (1.0 - gate), 0.0)
    ot[...] = ot[...] * inverse
    wide[...] = ot[...].T
    loads[2].wait()
    acc = jnp.zeros((cap, 128), F32)
    for h in range(heads):
        rows, lanes = slice(h * cap, (h + 1) * cap), slice(h * 128, (h + 1) * 128)
        o = wide[rows, :]
        up = g[:, lanes].astype(F32)
        branch[:, lanes] = (o * weight).astype(BF16)
        acc = acc + up * o
        wide[rows, :] = up * weight
    gterm[0:8, :] = jnp.zeros((8, 256), F32)
    gterm[0:1, 0:cap] = jnp.sum(acc.T, axis=0, keepdims=True)
    gterm[1:2, 0:cap] = factor
    cot = (wide[...].T * inverse).astype(BF16)
    dotx[0:128, :] = cot
    cotf = cot.astype(F32)
    delta = -jnp.sum(cotf * ot[...], axis=0, keepdims=True)
    d1 = delta.astype(BF16).astype(F32)
    d2 = (delta - d1).astype(BF16).astype(F32)
    d3 = delta - d1 - d2
    dotx[128:256, :] = jnp.where(
        first == 0, d1, jnp.where(first == 1, d2, jnp.where(first == 2, d3, 0.0))).astype(BF16)
    dob[...] = cotf.T.astype(BF16)

    def back(sl, start):
        e = e_scr[sl, :]
        ds = e * dot_nn(vx[sl, :], dotx[...]).astype(BF16)
        add = dot_tn(kx[sl, 0:128], ds)
        wide_t = ot
        wide_t[...] = add if start else wide_t[...] + add
        return dot_nn(ds, q[...]) * scale, dot_nn(e, dob[...])

    dk, dv = back(pl.ds(0, cap), True)
    own[:, 0:128] = dk
    own[:, 128:256] = dv

    def back_chunk(sl, rows, _):
        dk, dv = back(sl, False)
        dkv[sl, 0:128] = dk.astype(BF16)
        dkv[sl, 128:256] = dv.astype(BF16)
        return 0

    sweep(back_chunk, 0)
    row2 = lax.broadcasted_iota(jnp.int32, (cap, 256), 0)

    def block_store(s):
        return pltpu.make_async_copy(contrib.at[s % 2, s // 2], contrib_hbm.at[s % 2, s // 2], csem.at[s])

    def unplace(s, off):
        off = pl.multiple_of(off, 16)
        n = counts[s]
        block = dkv[pl.ds(off, cap), :].astype(F32)
        contrib[s % 2, s // 2] = jnp.where(row2 < n, block, 0.0).astype(BF16)
        block_store(s).start()
        return off + ((n + 15) // 16) * 16

    lax.fori_loop(0, me, unplace, cap)

    wide[...] = (ot[...] * scale).T
    for h in range(heads):
        dq[:, h * 128:(h + 1) * 128] = wide[h * cap:(h + 1) * cap, :].astype(BF16)

    def finish_store(s, _):
        block_store(s).wait()
        return 0

    lax.fori_loop(0, me, finish_store, 0)


def return_kernel(nseq, ntp, contrib, own_hbm, gterm, x_hbm, dkv_out, router_out,
                  half, own, x, lsem, pair, mine, inbox, inbox2, turn, part, gpair, gchip, sums, psem, prsem, ssem, rsem, s2sem, r2sem, tssem, trsem,
                  qsem, qrsem, gssem, grsem):
    me, mt = lax.axis_index("seq"), lax.axis_index("tp")
    nchip = nseq // 2
    chip, core = me // 2, me % 2
    sib = me + 1 - 2 * core
    cap = x.shape[0]
    loads = [
        pltpu.make_async_copy(contrib.at[core], half, lsem.at[0]),
        pltpu.make_async_copy(own_hbm, own, lsem.at[1]),
        pltpu.make_async_copy(x_hbm, x, lsem.at[2]),
    ]
    for load in loads:
        load.start()

    barrier = pltpu.get_barrier_semaphore()

    def greet_chip(c, _):
        @pl.when(c != chip)
        def _():
            pl.semaphore_signal(barrier, inc=1, device_id={"seq": 2 * c + core}, device_id_type=MESH)
        return 0

    def greet_tp(t, _):
        @pl.when(t != mt)
        def _():
            pl.semaphore_signal(barrier, inc=1, device_id={"tp": t}, device_id_type=MESH)
        return 0

    lax.fori_loop(0, nchip, greet_chip, 0)
    pl.semaphore_signal(barrier, inc=1, device_id={"seq": sib}, device_id_type=MESH)
    lax.fori_loop(0, ntp, greet_tp, 0)
    part[mt] = gterm[...]
    pl.semaphore_wait(barrier, nchip - 1 + 1 + ntp - 1)

    def tp_copy(slot, t):
        return pltpu.make_async_remote_copy(
            src_ref=part.at[slot], dst_ref=part.at[slot], send_sem=tssem.at[t], recv_sem=trsem.at[slot],
            device_id={"tp": t}, device_id_type=MESH)

    def send_tp(t, _):
        @pl.when(t != mt)
        def _():
            tp_copy(mt, t).start()
        return 0

    lax.fori_loop(0, ntp, send_tp, 0)

    def pair_copy(c):
        return pltpu.make_async_remote_copy(
            src_ref=contrib.at[1 - core, c], dst_ref=pair.at[c], send_sem=psem.at[c], recv_sem=prsem.at[c],
            device_id={"seq": sib}, device_id_type=MESH)

    def send_pair(c, _):
        @pl.when((c < chip) | ((c == chip) & (core == 1)))
        def _():
            pair_copy(c).start()
        return 0

    lax.fori_loop(0, nchip, send_pair, 0)

    grid = Grid(me, nchip)
    side, last = grid.side, grid.side - 1

    def first_copy(p, q):
        return pltpu.make_async_remote_copy(
            src_ref=mine.at[grid.at(p, q)], dst_ref=inbox.at[grid.a, q], send_sem=ssem.at[p * side + q],
            recv_sem=rsem.at[grid.a * side + q], device_id=grid.device(grid.at(p, grid.b)), device_id_type=MESH)

    def first_landed(p, q):
        return pltpu.make_async_remote_copy(
            src_ref=inbox.at[p, q], dst_ref=inbox.at[p, q], send_sem=ssem.at[p * side + q],
            recv_sem=rsem.at[p * side + q], device_id=grid.device(grid.at(p, grid.b)), device_id_type=MESH)

    def second_copy(q):
        return pltpu.make_async_remote_copy(
            src_ref=turn.at[q], dst_ref=inbox2.at[grid.b], send_sem=s2sem.at[q], recv_sem=r2sem.at[grid.b],
            device_id=grid.device(grid.at(grid.a, q)), device_id_type=MESH)

    def second_landed(q):
        return pltpu.make_async_remote_copy(
            src_ref=inbox2.at[q], dst_ref=inbox2.at[q], send_sem=s2sem.at[q], recv_sem=r2sem.at[q],
            device_id=grid.device(grid.at(grid.a, q)), device_id_type=MESH)

    loads[0].wait()

    def join(c):
        pair_copy(c).wait_recv()
        mine[c] = (half[c].astype(F32) + pair[c].astype(F32)).astype(BF16)

    for p in range(side):
        for q in range(side):
            @pl.when((p != grid.a) & (grid.at(p, q) < chip))
            def _():
                join(grid.at(p, q))
                first_copy(p, q).start()

    for q in range(side):
        @pl.when(grid.at(grid.a, q) < chip)
        def _():
            join(grid.at(grid.a, q))

    def wait_tp(t, _):
        @pl.when(t != mt)
        def _():
            tp_copy(t, t).wait_recv()
        return 0

    lax.fori_loop(0, ntp, wait_tp, 0)
    total = part[0, 0:1, :]
    for t in range(1, ntp):
        total = total + part[t, 0:1, :]
    dlogit = (total * gterm[1:2, :])[:, 0:cap]
    p1 = dlogit.astype(BF16)
    r1 = dlogit - p1.astype(F32)
    p2 = r1.astype(BF16)
    p3 = (r1 - p2.astype(F32)).astype(BF16)
    loads[2].wait()
    xs = x[...]
    share = (dot_nn(jnp.broadcast_to(p1, (16, cap)), xs) + dot_nn(jnp.broadcast_to(p2, (16, cap)), xs)
             + dot_nn(jnp.broadcast_to(p3, (16, cap)), xs))
    for i in range(x.shape[1] // 128):
        gpair[core, i:i + 1, :] = share[0:1, i * 128:(i + 1) * 128]

    def gpair_copy(slot):
        return pltpu.make_async_remote_copy(
            src_ref=gpair.at[slot], dst_ref=gpair.at[slot], send_sem=qsem, recv_sem=qrsem,
            device_id={"seq": sib}, device_id_type=MESH)

    gpair_copy(core).start()

    def finish_pair(c, _):
        @pl.when((c < chip) | ((c == chip) & (core == 1)))
        def _():
            pair_copy(c).wait_send()
        return 0

    lax.fori_loop(0, nchip, finish_pair, 0)

    def finish_tp(t, _):
        @pl.when(t != mt)
        def _():
            tp_copy(mt, t).wait_send()
        return 0

    lax.fori_loop(0, ntp, finish_tp, 0)
    gpair_copy(1 - core).wait_recv()
    gchip[chip] = gpair[0] + gpair[1]

    def gchip_copy(slot, c):
        return pltpu.make_async_remote_copy(
            src_ref=gchip.at[slot], dst_ref=gchip.at[slot], send_sem=gssem.at[c], recv_sem=grsem.at[slot],
            device_id={"seq": 2 * c + core}, device_id_type=MESH)

    def send_gchip(c, _):
        @pl.when(c != chip)
        def _():
            gchip_copy(chip, c).start()
        return 0

    lax.fori_loop(0, nchip, send_gchip, 0)

    for q in range(side):
        target = grid.at(grid.a, q)

        @pl.when((q != grid.b) & (target < grid.at(last, grid.b)))
        def _():
            @pl.when(target < chip)
            def _():
                sums[...] = mine[target].astype(F32)

            @pl.when(target >= chip)
            def _():
                sums[...] = jnp.zeros((cap, 256), F32)

            for p in range(side):
                @pl.when((p != grid.a) & (target < grid.at(p, grid.b)))
                def _():
                    first_landed(p, q).wait_recv()
                    sums[...] = sums[...] + inbox[p, q].astype(F32)
            turn[q] = sums[...].astype(BF16)
            second_copy(q).start()

    for q in range(side):
        for p in range(side):
            @pl.when((p != grid.a) & (grid.at(p, q) < chip))
            def _():
                first_copy(p, q).wait_send()

    def finish_gchip(c, _):
        @pl.when(c != chip)
        def _():
            gchip_copy(chip, c).wait_send()
        return 0

    lax.fori_loop(0, nchip, finish_gchip, 0)

    @pl.when(core == 0)
    def _():
        pair_copy(chip).wait_recv()
        pair[nchip] = pair[chip]

    @pl.when(core == 1)
    def _():
        pair[nchip] = jnp.zeros((cap, 256), BF16)

    loads[1].wait()
    sums[...] = own[...] + pair[nchip].astype(F32)

    for p in range(side):
        @pl.when((p != grid.a) & (chip < grid.at(p, grid.b)))
        def _():
            first_landed(p, grid.b).wait_recv()
            sums[...] = sums[...] + inbox[p, grid.b].astype(F32)

    for q in range(side):
        @pl.when((q != grid.b) & (chip < grid.at(last, q)))
        def _():
            second_landed(q).wait_recv()
            sums[...] = sums[...] + inbox2[q].astype(F32)
    dkv_out[0] = sums[:, 0:128].astype(BF16)
    dkv_out[1] = sums[:, 128:256].astype(BF16)

    def wait_gchip(c, _):
        @pl.when(c != chip)
        def _():
            gchip_copy(c, c).wait_recv()
        return 0

    lax.fori_loop(0, nchip, wait_gchip, 0)
    total = gchip[0]
    for c in range(1, nchip):
        total = total + gchip[c]
    router_out[...] = total

    gpair_copy(core).wait_send()
    for q in range(side):
        @pl.when((q != grid.b) & (grid.at(grid.a, q) < grid.at(last, grid.b)))
        def _():
            second_copy(q).wait_send()


def vmem(n=1):
    specs = [pl.BlockSpec(memory_space=pltpu.VMEM) for _ in range(n)]
    return specs if n > 1 else specs[0]


def shards(hidden, queries, keys_values, w_router, routed, counts, grad_out):
    nseq, ntp = lax.axis_size("seq"), lax.axis_size("tp")
    nchip = nseq // 2
    side = math.isqrt(nchip)
    cap = routed.shape[1]
    tok, width = queries.shape
    heads = width // HEAD_WIDTH
    nq = heads * cap
    scale = 1.0 / math.sqrt(HEAD_WIDTH)
    dma, shape = pltpu.SemaphoreType.DMA, jax.ShapeDtypeStruct
    anywhere = pl.BlockSpec(memory_space=pl.ANY)

    x, q, kvall, logit = pl.pallas_call(
        functools.partial(fetch_kernel, nseq, ntp),
        out_shape=(shape((cap, width), BF16), shape((heads, cap, 128), BF16),
                   shape((nseq, cap, 256), BF16), shape((8, 256), F32)),
        in_specs=[anywhere] * 3 + vmem(2),
        out_specs=tuple(vmem(2)) + (anywhere, vmem()),
        scratch_shapes=[
            pltpu.VMEM((tok, width), BF16), pltpu.VMEM((tok, width), BF16), pltpu.VMEM((2, tok, 128), BF16),
            pltpu.VMEM((cap, 256), BF16), pltpu.VMEM((ntp, 8, 256), F32), dma((4,)), dma((nchip,)), dma((nchip,)), dma((nchip,)), dma((nchip,)),
            dma((nchip,)), dma((ntp,)), dma((ntp,)),
        ],
        compiler_params=pltpu.CompilerParams(
            collective_id=0, has_side_effects=True, vmem_limit_bytes=VMEM_LIMIT),
        name="fetch",
    )(hidden, queries, keys_values, w_router, routed)

    live = nseq * cap * LIVE_SHARE[0] // LIVE_SHARE[1]
    span = -(-(live + 15 * nseq) // CHUNK) * CHUNK
    rows = cap + span + CHUNK
    branch, dq, contrib, own, gterm = pl.pallas_call(
        functools.partial(attend_kernel, scale),
        out_shape=(shape((cap, width), BF16), shape((cap, width), BF16),
                   shape((2, nchip, cap, 256), BF16), shape((cap, 256), F32), shape((8, 256), F32)),
        in_specs=[pl.BlockSpec(memory_space=pltpu.SMEM)] + [anywhere] * 3 + [vmem()],
        out_specs=tuple(vmem(2)) + (anywhere,) + tuple(vmem(2)),
        scratch_shapes=[
            pltpu.VMEM((nseq, cap, 256), BF16), pltpu.VMEM((nq, 128), BF16), pltpu.VMEM((cap, width), BF16),
            pltpu.VMEM((2, nchip, cap, 256), BF16), dma((3,)), dma((nseq,)),
            pltpu.VMEM((rows, 256), BF16), pltpu.VMEM((rows, 256), BF16),
            pltpu.VMEM((256, nq), BF16), pltpu.VMEM((256, nq), BF16), pltpu.VMEM((nq, 128), BF16),
            pltpu.VMEM((cap + span, nq), F32), pltpu.VMEM((cap + span, nq), BF16),
            pltpu.VMEM((128, nq), F32), pltpu.VMEM((nq, 128), F32), pltpu.VMEM((rows, 256), BF16),
        ],
        compiler_params=pltpu.CompilerParams(vmem_limit_bytes=VMEM_LIMIT),
        name="attend",
    )(counts, kvall, q.reshape(nq, 128), grad_out, logit)

    dkv, router = pl.pallas_call(
        functools.partial(return_kernel, nseq, ntp),
        out_shape=(shape((2, cap, 128), BF16), shape((width // 128, 128), F32)),
        in_specs=[anywhere, anywhere, vmem(), anywhere],
        out_specs=tuple(vmem(2)),
        scratch_shapes=[
            pltpu.VMEM((nchip, cap, 256), BF16), pltpu.VMEM((cap, 256), F32), pltpu.VMEM((cap, width), BF16), dma((3,)),
            pltpu.VMEM((nchip + 1, cap, 256), BF16), pltpu.VMEM((nchip, cap, 256), BF16),
            pltpu.VMEM((side, side, cap, 256), BF16), pltpu.VMEM((side, cap, 256), BF16),
            pltpu.VMEM((side, cap, 256), BF16), pltpu.VMEM((ntp, 8, 256), F32),
            pltpu.VMEM((2, width // 128, 128), F32), pltpu.VMEM((nchip, width // 128, 128), F32), pltpu.VMEM((cap, 256), F32),
            dma((nchip,)), dma((nchip,)), dma((nchip,)), dma((nchip,)), dma((side,)), dma((side,)), dma((ntp,)), dma((ntp,)),
            dma, dma, dma((nchip,)), dma((nchip,)),
        ],
        compiler_params=pltpu.CompilerParams(
            collective_id=1, has_side_effects=True, vmem_limit_bytes=VMEM_LIMIT),
        name="settle",
    )(contrib, own, gterm, x)
    return branch, dq, dkv, router.reshape(width)


def solution(mesh):
    in_specs = (
        P("seq", "tp"),
        P("seq", "tp"),
        P(None, "seq", "tp"),
        P("tp"),
        P("seq", None),
        P(),
        P("seq", "tp"),
    )
    out_specs = (P("seq", "tp"), P("seq", "tp"), P(None, "seq", "tp"), P("tp"))
    return jax.shard_map(shards, mesh=mesh, in_specs=in_specs, out_specs=out_specs, check_vma=False)
```

```python
import functools
import math

import jax
import jax.numpy as jnp
from jax import lax
from jax.experimental import pallas as pl
from jax.experimental.pallas import tpu as pltpu
from jax.sharding import PartitionSpec as P

HEAD_WIDTH = 128
MESH = pl.DeviceIdType.MESH
NEG = -1e30
VMEM_LIMIT = 62 * 2 ** 20
CHUNK = 256
LIVE_SHARE = (5, 8)
F32 = jnp.float32
BF16 = jnp.bfloat16


def dot_nn(a, b):
    return lax.dot_general(a, b, (((1,), (0,)), ((), ())), preferred_element_type=F32)


def dot_nt(a, b):
    return lax.dot_general(a, b, (((1,), (1,)), ((), ())), preferred_element_type=F32)


def dot_tn(a, b):
    return lax.dot_general(a, b, (((0,), (0,)), ((), ())), preferred_element_type=F32)


def rows_of(row, cap):
    return jnp.broadcast_to(row, (128, cap)).T


class Grid:
    def __init__(self, me, nchip):
        self.side = math.isqrt(nchip)
        self.chip, self.core = me // 2, me % 2
        self.sib = me + 1 - 2 * self.core
        high, low = self.chip // self.side, self.chip % self.side
        self.a = jnp.where(self.core == 0, high, low)
        self.b = jnp.where(self.core == 0, low, high)

    def at(self, a, b):
        return jnp.where(self.core == 0, self.side * a + b, self.side * b + a)

    def device(self, chip):
        return {"seq": 2 * chip + self.core}


def fetch_kernel(nseq, ntp, hid, qry, kv, w, routed, x_out, q_out, kvall, logit_out,
                 hid_v, qry_v, kv_v, held, part, lsem, ssem, ssem2, rsem, fsem, gsem, tssem, trsem):
    me, mt = lax.axis_index("seq"), lax.axis_index("tp")
    nchip = nseq // 2
    chip, core = me // 2, me % 2
    sib = me + 1 - 2 * core
    cap = routed.shape[1]
    tok = hid.shape[0]
    heads = q_out.shape[0]
    load_kv = pltpu.make_async_copy(kv, kv_v, lsem.at[0])
    load_hid = pltpu.make_async_copy(hid, hid_v, lsem.at[1])
    load_qry = pltpu.make_async_copy(qry, qry_v, lsem.at[2])
    load_kv.start()

    barrier = pltpu.get_barrier_semaphore()

    grid = Grid(me, nchip)
    side, last = grid.side, grid.side - 1
    for q in range(side):
        @pl.when(q != grid.b)
        def _():
            pl.semaphore_signal(barrier, inc=1, device_id=grid.device(grid.at(grid.a, q)), device_id_type=MESH)

        @pl.when(q != grid.a)
        def _():
            pl.semaphore_signal(barrier, inc=1, device_id=grid.device(grid.at(q, grid.b)), device_id_type=MESH)

    def greet_tp(t, _):
        @pl.when(t != mt)
        def _():
            pl.semaphore_signal(barrier, inc=1, device_id={"tp": t}, device_id_type=MESH)
        return 0

    pl.semaphore_signal(barrier, inc=1, device_id={"seq": sib}, device_id_type=MESH)
    lax.fori_loop(0, ntp, greet_tp, 0)

    col = rows_of(routed[...].astype(F32), cap)
    lane = lax.broadcasted_iota(jnp.int32, (cap, 128), 1).astype(F32)
    onehot = jnp.concatenate(
        [jnp.where(col == lane + 128.0 * j, 1.0, 0.0).astype(BF16) for j in range(tok // 128)], axis=1
    )
    load_kv.wait()
    load_hid.start()
    load_qry.start()
    held[:, 0:128] = dot_nn(onehot, kv_v[0]).astype(BF16)
    held[:, 128:256] = dot_nn(onehot, kv_v[1]).astype(BF16)
    keep = pltpu.make_async_copy(held, kvall.at[me], lsem.at[3])
    keep.start()

    pl.semaphore_wait(barrier, 2 * last + 1 + ntp - 1)

    def to_line(q):
        return pltpu.make_async_remote_copy(
            src_ref=held, dst_ref=kvall.at[me], send_sem=ssem.at[q], recv_sem=rsem.at[chip],
            device_id=grid.device(grid.at(grid.a, q)), device_id_type=MESH)

    def line_used(q):
        return (q != grid.b) & (chip < grid.at(last, q))

    def own_to_sib():
        return pltpu.make_async_remote_copy(
            src_ref=held, dst_ref=kvall.at[me], send_sem=fsem.at[chip], recv_sem=gsem.at[chip],
            device_id={"seq": sib}, device_id_type=MESH)

    def across(p, q):
        c = grid.at(grid.a, q)
        block = kvall.at[2 * c + core]
        return pltpu.make_async_remote_copy(
            src_ref=block, dst_ref=block, send_sem=ssem2.at[p * side + q], recv_sem=rsem.at[c],
            device_id=grid.device(grid.at(p, grid.b)), device_id_type=MESH)

    def own_across(p):
        return pltpu.make_async_remote_copy(
            src_ref=held, dst_ref=kvall.at[me], send_sem=ssem2.at[p * side + grid.b], recv_sem=rsem.at[chip],
            device_id=grid.device(grid.at(p, grid.b)), device_id_type=MESH)

    def across_used(p, q):
        return (p != grid.a) & (grid.at(grid.a, q) < grid.at(p, grid.b))

    for q in range(side):
        @pl.when(line_used(q))
        def _():
            to_line(q).start()

    for p in range(side):
        @pl.when(across_used(p, grid.b))
        def _():
            own_across(p).start()

    @pl.when(core == 0)
    def _():
        own_to_sib().start()

    def landed(c):
        block = kvall.at[2 * c + core]
        return pltpu.make_async_remote_copy(
            src_ref=block, dst_ref=block, send_sem=fsem.at[c], recv_sem=rsem.at[c],
            device_id={"seq": sib}, device_id_type=MESH)

    def forward(c):
        block = kvall.at[2 * c + core]
        return pltpu.make_async_remote_copy(
            src_ref=block, dst_ref=block, send_sem=fsem.at[c], recv_sem=gsem.at[c],
            device_id={"seq": sib}, device_id_type=MESH)

    def forwarded(c):
        block = kvall.at[2 * c + 1 - core]
        return pltpu.make_async_remote_copy(
            src_ref=block, dst_ref=block, send_sem=fsem.at[c], recv_sem=gsem.at[c],
            device_id={"seq": sib}, device_id_type=MESH)

    load_hid.wait()
    x = dot_nn(onehot, hid_v[...]).astype(BF16)
    x_out[...] = x
    logit = dot_nt(jnp.broadcast_to(w[...].reshape(1, w.shape[0]), (16, w.shape[0])), x)
    part[mt, :, :] = jnp.zeros((8, 256), F32)
    part[mt, :, 0:cap] = logit[0:8]

    def to_tp(t):
        return pltpu.make_async_remote_copy(
            src_ref=part.at[mt], dst_ref=part.at[mt], send_sem=tssem.at[t], recv_sem=trsem.at[mt],
            device_id={"tp": t}, device_id_type=MESH)

    def from_tp(t):
        return pltpu.make_async_remote_copy(
            src_ref=part.at[t], dst_ref=part.at[t], send_sem=tssem.at[t], recv_sem=trsem.at[t],
            device_id={"tp": t}, device_id_type=MESH)

    def send_tp(t, _):
        @pl.when(t != mt)
        def _():
            to_tp(t).start()
        return 0

    lax.fori_loop(0, ntp, send_tp, 0)

    for q in range(side):
        c = grid.at(grid.a, q)

        @pl.when((q != grid.b) & (c < grid.at(last, grid.b)))
        def _():
            landed(c).wait_recv()

            for p in range(side):
                @pl.when(across_used(p, q))
                def _():
                    across(p, q).start()

            @pl.when(c < chip)
            def _():
                forward(c).start()

    load_qry.wait()
    for h in range(heads):
        q_out[h] = dot_nn(onehot, qry_v[:, h * 128:(h + 1) * 128]).astype(BF16)

    def wait_tp(t, _):
        @pl.when(t != mt)
        def _():
            from_tp(t).wait_recv()
        return 0

    lax.fori_loop(0, ntp, wait_tp, 0)
    total = part[0]
    for t in range(1, ntp):
        total = total + part[t]
    logit_out[...] = total

    for step in range(1, side):
        for q in range(side):
            c = grid.at(lax.rem(grid.a - step + side, side), q)

            @pl.when(c < chip)
            def _():
                landed(c).wait_recv()
                forward(c).start()

    for q in range(side):
        @pl.when(line_used(q))
        def _():
            to_line(q).wait_send()

    keep.wait()

    @pl.when(core == 0)
    def _():
        own_to_sib().wait_send()

    def finish_tp(t, _):
        @pl.when(t != mt)
        def _():
            to_tp(t).wait_send()
        return 0

    lax.fori_loop(0, ntp, finish_tp, 0)
    for q in range(side):
        for p in range(side):
            @pl.when(across_used(p, q))
            def _():
                across(p, q).wait_send()

    def finish_send(c, _):
        @pl.when(c < chip)
        def _():
            forward(c).wait_send()
        return 0

    def finish(c, _):
        @pl.when(c < chip)
        def _():
            forwarded(c).wait_recv()
        return 0

    lax.fori_loop(0, nchip, finish_send, 0)

    @pl.when(core == 1)
    def _():
        forwarded(chip).wait_recv()

    lax.fori_loop(0, nchip, finish, 0)


def attend_kernel(scale, counts, kv_hbm, q_hbm, g_hbm, logit, branch, dq, contrib_hbm, own, gterm,
                  kvall, q, g, contrib, lsem, csem, kx, vx, qtx, dotx, dob, s_scr, e_scr, ot, wide, dkv):
    me = lax.axis_index("seq")
    cap, width = g.shape
    nq = q.shape[0]
    heads = width // 128
    to_exp2 = scale * math.log2(math.e)
    live_here = counts[me]
    loads = [
        pltpu.make_async_copy(kv_hbm.at[me], kvall.at[me], lsem.at[0]),
        pltpu.make_async_copy(q_hbm, q, lsem.at[1]),
        pltpu.make_async_copy(g_hbm, g, lsem.at[2]),
    ]
    for load in loads:
        load.start()

    def block_load(s):
        return pltpu.make_async_copy(kv_hbm.at[s], kvall.at[s], csem.at[s])

    def start_load(s, _):
        block_load(s).start()
        return 0

    lax.fori_loop(0, me, start_load, 0)

    row = lax.broadcasted_iota(jnp.int32, (cap, 128), 0)
    lane = lax.broadcasted_iota(jnp.int32, (cap, 128), 1)
    ones3 = jnp.where(lane < 3, 1.0, 0.0).astype(BF16)
    loads[0].wait()
    kx[0:cap, 0:128] = kvall[me, :, 0:128]
    kx[0:cap, 128:256] = jnp.zeros((cap, 128), BF16)
    vx[0:cap, 0:128] = kvall[me, :, 128:256]
    vx[0:cap, 128:256] = ones3

    def place(s, off):
        block_load(s).wait()
        off = pl.multiple_of(off, 16)
        n = counts[s]
        kx[pl.ds(off, cap), 0:128] = kvall[s, :, 0:128]
        kx[pl.ds(off, cap), 128:256] = jnp.where((row >= n) & (lane == 0), NEG, 0.0).astype(BF16)
        vx[pl.ds(off, cap), 0:128] = kvall[s, :, 128:256]
        vx[pl.ds(off, cap), 128:256] = ones3
        return off + ((n + 15) // 16) * 16

    end = pl.multiple_of(lax.fori_loop(0, me, place, cap), 16)
    kx[pl.ds(end, CHUNK), 0:128] = jnp.zeros((CHUNK, 128), BF16)
    kx[pl.ds(end, CHUNK), 128:256] = jnp.where(
        lax.broadcasted_iota(jnp.int32, (CHUNK, 128), 1) == 0, NEG, 0.0).astype(BF16)
    vx[pl.ds(end, CHUNK), :] = jnp.zeros((CHUNK, 256), BF16)
    chunks = (end - cap + CHUNK - 1) // CHUNK
    doubles = chunks // 2

    def at(c, size):
        return pl.ds(pl.multiple_of(cap + c * CHUNK, 32), size * CHUNK)

    def sweep(step, carry):
        quads = chunks // 4
        carry = lax.fori_loop(0, quads, lambda c, held: step(at(4 * c, 4), 4 * CHUNK, held), carry)
        carry = lax.fori_loop(
            2 * quads, doubles, lambda c, held: step(at(2 * c, 2), 2 * CHUNK, held), carry)
        return lax.fori_loop(2 * doubles, chunks, lambda c, held: step(at(c, 1), CHUNK, held), carry)

    loads[1].wait()

    qtx[0:128, :] = q[...].T
    first = lax.broadcasted_iota(jnp.int32, (128, nq), 0)
    qtx[128:256, :] = jnp.where(first == 0, 1.0, 0.0).astype(BF16)

    key_slot = lax.broadcasted_iota(jnp.int32, (cap, nq), 0)
    pos = lax.broadcasted_iota(jnp.int32, (cap, nq), 1)
    query_slot = pos
    for h in range(1, heads):
        query_slot = query_slot - jnp.where(pos >= h * cap, cap, 0)
    s = jnp.where(key_slot <= query_slot, dot_nn(kx[0:cap, :], qtx[...]), NEG)
    s_scr[0:cap, :] = s
    top = jnp.max(s.reshape(cap // 8, 8, nq), axis=0)

    def score(sl, rows, top):
        s = dot_nn(kx[sl, :], qtx[...])
        s_scr[sl, :] = s
        return jnp.maximum(top, jnp.max(s.reshape(rows // 8, 8, nq), axis=0))

    top = sweep(score, top)
    top = jnp.max(top, axis=0, keepdims=True) * to_exp2

    def soften(sl, rows, total, start):
        e = jnp.exp2(s_scr[sl, :] * to_exp2 - top)
        eb = e.astype(BF16)
        e_scr[sl, :] = eb
        add = dot_tn(vx[sl, 0:128], eb)
        ot[...] = add if start else ot[...] + add
        return total + jnp.sum(e.reshape(rows // 8, 8, nq), axis=0)

    total = soften(pl.ds(0, cap), cap, jnp.zeros((8, nq), F32), True)
    total = sweep(lambda sl, rows, t: soften(sl, rows, t, False), total)
    inverse = 1.0 / jnp.sum(total, axis=0, keepdims=True)

    z = logit[0:1, 0:cap]
    gate = 1.0 / (1.0 + jnp.exp(-z))
    live = lax.broadcasted_iota(jnp.int32, (1, cap), 1) < live_here
    weight = rows_of(jnp.where(live, gate, 0.0), cap)
    factor = jnp.where(live, gate * (1.0 - gate), 0.0)
    ot[...] = ot[...] * inverse
    wide[...] = ot[...].T
    loads[2].wait()
    acc = jnp.zeros((cap, 128), F32)
    for h in range(heads):
        rows, lanes = slice(h * cap, (h + 1) * cap), slice(h * 128, (h + 1) * 128)
        o = wide[rows, :]
        up = g[:, lanes].astype(F32)
        branch[:, lanes] = (o * weight).astype(BF16)
        acc = acc + up * o
        wide[rows, :] = up * weight
    gterm[0:8, :] = jnp.zeros((8, 256), F32)
    gterm[0:1, 0:cap] = jnp.sum(acc.T, axis=0, keepdims=True)
    gterm[1:2, 0:cap] = factor
    cot = (wide[...].T * inverse).astype(BF16)
    dotx[0:128, :] = cot
    cotf = cot.astype(F32)
    delta = -jnp.sum(cotf * ot[...], axis=0, keepdims=True)
    d1 = delta.astype(BF16).astype(F32)
    d2 = (delta - d1).astype(BF16).astype(F32)
    d3 = delta - d1 - d2
    dotx[128:256, :] = jnp.where(
        first == 0, d1, jnp.where(first == 1, d2, jnp.where(first == 2, d3, 0.0))).astype(BF16)
    dob[...] = cotf.T.astype(BF16)

    def back(sl, start):
        e = e_scr[sl, :]
        ds = e * dot_nn(vx[sl, :], dotx[...]).astype(BF16)
        add = dot_tn(kx[sl, 0:128], ds)
        wide_t = ot
        wide_t[...] = add if start else wide_t[...] + add
        return dot_nn(ds, q[...]) * scale, dot_nn(e, dob[...])

    dk, dv = back(pl.ds(0, cap), True)
    own[:, 0:128] = dk
    own[:, 128:256] = dv

    def back_chunk(sl, rows, _):
        dk, dv = back(sl, False)
        dkv[sl, 0:128] = dk.astype(BF16)
        dkv[sl, 128:256] = dv.astype(BF16)
        return 0

    sweep(back_chunk, 0)
    row2 = lax.broadcasted_iota(jnp.int32, (cap, 256), 0)

    def block_store(s):
        return pltpu.make_async_copy(contrib.at[s % 2, s // 2], contrib_hbm.at[s % 2, s // 2], csem.at[s])

    def unplace(s, off):
        off = pl.multiple_of(off, 16)
        n = counts[s]
        block = dkv[pl.ds(off, cap), :].astype(F32)
        contrib[s % 2, s // 2] = jnp.where(row2 < n, block, 0.0).astype(BF16)
        block_store(s).start()
        return off + ((n + 15) // 16) * 16

    lax.fori_loop(0, me, unplace, cap)

    wide[...] = (ot[...] * scale).T
    for h in range(heads):
        dq[:, h * 128:(h + 1) * 128] = wide[h * cap:(h + 1) * cap, :].astype(BF16)

    def finish_store(s, _):
        block_store(s).wait()
        return 0

    lax.fori_loop(0, me, finish_store, 0)


def return_kernel(nseq, ntp, contrib, own_hbm, gterm, x_hbm, dkv_out, router_out,
                  half, own, x, lsem, pair, mine, inbox, inbox2, turn, part, gpair, gchip, sums, psem, prsem, ssem, rsem, s2sem, r2sem, tssem, trsem,
                  qsem, qrsem, gssem, grsem):
    me, mt = lax.axis_index("seq"), lax.axis_index("tp")
    nchip = nseq // 2
    chip, core = me // 2, me % 2
    sib = me + 1 - 2 * core
    cap = x.shape[0]
    loads = [
        pltpu.make_async_copy(contrib.at[core], half, lsem.at[0]),
        pltpu.make_async_copy(own_hbm, own, lsem.at[1]),
        pltpu.make_async_copy(x_hbm, x, lsem.at[2]),
    ]
    for load in loads:
        load.start()

    barrier = pltpu.get_barrier_semaphore()

    def greet_chip(c, _):
        @pl.when(c != chip)
        def _():
            pl.semaphore_signal(barrier, inc=1, device_id={"seq": 2 * c + core}, device_id_type=MESH)
        return 0

    def greet_tp(t, _):
        @pl.when(t != mt)
        def _():
            pl.semaphore_signal(barrier, inc=1, device_id={"tp": t}, device_id_type=MESH)
        return 0

    lax.fori_loop(0, nchip, greet_chip, 0)
    pl.semaphore_signal(barrier, inc=1, device_id={"seq": sib}, device_id_type=MESH)
    lax.fori_loop(0, ntp, greet_tp, 0)
    part[mt] = gterm[...]
    pl.semaphore_wait(barrier, nchip - 1 + 1 + ntp - 1)

    def tp_copy(slot, t):
        return pltpu.make_async_remote_copy(
            src_ref=part.at[slot], dst_ref=part.at[slot], send_sem=tssem.at[t], recv_sem=trsem.at[slot],
            device_id={"tp": t}, device_id_type=MESH)

    def send_tp(t, _):
        @pl.when(t != mt)
        def _():
            tp_copy(mt, t).start()
        return 0

    lax.fori_loop(0, ntp, send_tp, 0)

    side0 = math.isqrt(nchip)

    def pair_copy(c):
        return pltpu.make_async_remote_copy(
            src_ref=contrib.at[1 - core, c], dst_ref=pair.at[c], send_sem=psem.at[c], recv_sem=prsem.at[c],
            device_id={"seq": sib}, device_id_type=MESH)

    def send_pair(i, _):
        c = jnp.where(core == 0, i % side0 * side0 + i // side0, i)

        @pl.when((c < chip) | ((c == chip) & (core == 1)))
        def _():
            pair_copy(c).start()
        return 0

    lax.fori_loop(0, nchip, send_pair, 0)

    grid = Grid(me, nchip)
    side, last = grid.side, grid.side - 1

    def first_copy(p, q):
        return pltpu.make_async_remote_copy(
            src_ref=mine.at[grid.at(p, q)], dst_ref=inbox.at[grid.a, q], send_sem=ssem.at[p * side + q],
            recv_sem=rsem.at[grid.a * side + q], device_id=grid.device(grid.at(p, grid.b)), device_id_type=MESH)

    def first_landed(p, q):
        return pltpu.make_async_remote_copy(
            src_ref=inbox.at[p, q], dst_ref=inbox.at[p, q], send_sem=ssem.at[p * side + q],
            recv_sem=rsem.at[p * side + q], device_id=grid.device(grid.at(p, grid.b)), device_id_type=MESH)

    def second_copy(q):
        return pltpu.make_async_remote_copy(
            src_ref=turn.at[q], dst_ref=inbox2.at[grid.b], send_sem=s2sem.at[q], recv_sem=r2sem.at[grid.b],
            device_id=grid.device(grid.at(grid.a, q)), device_id_type=MESH)

    def second_landed(q):
        return pltpu.make_async_remote_copy(
            src_ref=inbox2.at[q], dst_ref=inbox2.at[q], send_sem=s2sem.at[q], recv_sem=r2sem.at[q],
            device_id=grid.device(grid.at(grid.a, q)), device_id_type=MESH)

    loads[0].wait()

    def join(c):
        pair_copy(c).wait_recv()
        mine[c] = (half[c].astype(F32) + pair[c].astype(F32)).astype(BF16)

    for p in range(side):
        for q in range(side):
            @pl.when((p != grid.a) & (grid.at(p, q) < chip))
            def _():
                join(grid.at(p, q))
                first_copy(p, q).start()

    for q in range(side):
        @pl.when(grid.at(grid.a, q) < chip)
        def _():
            join(grid.at(grid.a, q))

    def wait_tp(t, _):
        @pl.when(t != mt)
        def _():
            tp_copy(t, t).wait_recv()
        return 0

    lax.fori_loop(0, ntp, wait_tp, 0)
    total = part[0, 0:1, :]
    for t in range(1, ntp):
        total = total + part[t, 0:1, :]
    dlogit = (total * gterm[1:2, :])[:, 0:cap]
    p1 = dlogit.astype(BF16)
    r1 = dlogit - p1.astype(F32)
    p2 = r1.astype(BF16)
    p3 = (r1 - p2.astype(F32)).astype(BF16)
    loads[2].wait()
    xs = x[...]
    rows16 = lax.broadcasted_iota(jnp.int32, (16, cap), 0)
    parts = jnp.where(rows16 == 0, p1.astype(F32), jnp.where(
        rows16 == 1, p2.astype(F32), jnp.where(rows16 == 2, p3.astype(F32), 0.0))).astype(BF16)
    share = jnp.sum(dot_nn(parts, xs), axis=0, keepdims=True)
    for i in range(x.shape[1] // 128):
        gpair[core, i:i + 1, :] = share[0:1, i * 128:(i + 1) * 128]

    def gpair_copy(slot):
        return pltpu.make_async_remote_copy(
            src_ref=gpair.at[slot], dst_ref=gpair.at[slot], send_sem=qsem, recv_sem=qrsem,
            device_id={"seq": sib}, device_id_type=MESH)

    gpair_copy(core).start()

    def finish_pair(c, _):
        @pl.when((c < chip) | ((c == chip) & (core == 1)))
        def _():
            pair_copy(c).wait_send()
        return 0

    lax.fori_loop(0, nchip, finish_pair, 0)

    def finish_tp(t, _):
        @pl.when(t != mt)
        def _():
            tp_copy(mt, t).wait_send()
        return 0

    lax.fori_loop(0, ntp, finish_tp, 0)
    gpair_copy(1 - core).wait_recv()
    gchip[chip] = gpair[0] + gpair[1]

    def gchip_copy(slot, c):
        return pltpu.make_async_remote_copy(
            src_ref=gchip.at[slot], dst_ref=gchip.at[slot], send_sem=gssem.at[c], recv_sem=grsem.at[slot],
            device_id={"seq": 2 * c + core}, device_id_type=MESH)

    def send_gchip(c, _):
        @pl.when(c != chip)
        def _():
            gchip_copy(chip, c).start()
        return 0

    lax.fori_loop(0, nchip, send_gchip, 0)

    for q in range(side):
        target = grid.at(grid.a, q)

        @pl.when((q != grid.b) & (target < grid.at(last, grid.b)))
        def _():
            @pl.when(target < chip)
            def _():
                sums[...] = mine[target].astype(F32)

            @pl.when(target >= chip)
            def _():
                sums[...] = jnp.zeros((cap, 256), F32)

            for p in range(side):
                @pl.when((p != grid.a) & (target < grid.at(p, grid.b)))
                def _():
                    first_landed(p, q).wait_recv()
                    sums[...] = sums[...] + inbox[p, q].astype(F32)
            turn[q] = sums[...].astype(BF16)
            second_copy(q).start()

    for q in range(side):
        for p in range(side):
            @pl.when((p != grid.a) & (grid.at(p, q) < chip))
            def _():
                first_copy(p, q).wait_send()

    def finish_gchip(c, _):
        @pl.when(c != chip)
        def _():
            gchip_copy(chip, c).wait_send()
        return 0

    lax.fori_loop(0, nchip, finish_gchip, 0)

    @pl.when(core == 0)
    def _():
        pair_copy(chip).wait_recv()
        pair[nchip] = pair[chip]

    @pl.when(core == 1)
    def _():
        pair[nchip] = jnp.zeros((cap, 256), BF16)

    loads[1].wait()
    sums[...] = own[...] + pair[nchip].astype(F32)

    for p in range(side):
        @pl.when((p != grid.a) & (chip < grid.at(p, grid.b)))
        def _():
            first_landed(p, grid.b).wait_recv()
            sums[...] = sums[...] + inbox[p, grid.b].astype(F32)

    for q in range(side):
        @pl.when((q != grid.b) & (chip < grid.at(last, q)))
        def _():
            second_landed(q).wait_recv()
            sums[...] = sums[...] + inbox2[q].astype(F32)
    dkv_out[0] = sums[:, 0:128].astype(BF16)
    dkv_out[1] = sums[:, 128:256].astype(BF16)

    def wait_gchip(c, _):
        @pl.when(c != chip)
        def _():
            gchip_copy(c, c).wait_recv()
        return 0

    lax.fori_loop(0, nchip, wait_gchip, 0)
    total = gchip[0]
    for c in range(1, nchip):
        total = total + gchip[c]
    router_out[...] = total

    gpair_copy(core).wait_send()
    for q in range(side):
        @pl.when((q != grid.b) & (grid.at(grid.a, q) < grid.at(last, grid.b)))
        def _():
            second_copy(q).wait_send()


def vmem(n=1):
    specs = [pl.BlockSpec(memory_space=pltpu.VMEM) for _ in range(n)]
    return specs if n > 1 else specs[0]


def shards(hidden, queries, keys_values, w_router, routed, counts, grad_out):
    nseq, ntp = lax.axis_size("seq"), lax.axis_size("tp")
    nchip = nseq // 2
    side = math.isqrt(nchip)
    cap = routed.shape[1]
    tok, width = queries.shape
    heads = width // HEAD_WIDTH
    nq = heads * cap
    scale = 1.0 / math.sqrt(HEAD_WIDTH)
    dma, shape = pltpu.SemaphoreType.DMA, jax.ShapeDtypeStruct
    anywhere = pl.BlockSpec(memory_space=pl.ANY)

    x, q, kvall, logit = pl.pallas_call(
        functools.partial(fetch_kernel, nseq, ntp),
        out_shape=(shape((cap, width), BF16), shape((heads, cap, 128), BF16),
                   shape((nseq, cap, 256), BF16), shape((8, 256), F32)),
        in_specs=[anywhere] * 3 + vmem(2),
        out_specs=tuple(vmem(2)) + (anywhere, vmem()),
        scratch_shapes=[
            pltpu.VMEM((tok, width), BF16), pltpu.VMEM((tok, width), BF16), pltpu.VMEM((2, tok, 128), BF16),
            pltpu.VMEM((cap, 256), BF16), pltpu.VMEM((ntp, 8, 256), F32), dma((4,)), dma((nchip,)), dma((nchip,)), dma((nchip,)), dma((nchip,)),
            dma((nchip,)), dma((ntp,)), dma((ntp,)),
        ],
        compiler_params=pltpu.CompilerParams(
            collective_id=0, has_side_effects=True, vmem_limit_bytes=VMEM_LIMIT),
        name="fetch",
    )(hidden, queries, keys_values, w_router, routed)

    live = nseq * cap * LIVE_SHARE[0] // LIVE_SHARE[1]
    span = -(-(live + 15 * nseq) // CHUNK) * CHUNK
    rows = cap + span + CHUNK
    branch, dq, contrib, own, gterm = pl.pallas_call(
        functools.partial(attend_kernel, scale),
        out_shape=(shape((cap, width), BF16), shape((cap, width), BF16),
                   shape((2, nchip, cap, 256), BF16), shape((cap, 256), F32), shape((8, 256), F32)),
        in_specs=[pl.BlockSpec(memory_space=pltpu.SMEM)] + [anywhere] * 3 + [vmem()],
        out_specs=tuple(vmem(2)) + (anywhere,) + tuple(vmem(2)),
        scratch_shapes=[
            pltpu.VMEM((nseq, cap, 256), BF16), pltpu.VMEM((nq, 128), BF16), pltpu.VMEM((cap, width), BF16),
            pltpu.VMEM((2, nchip, cap, 256), BF16), dma((3,)), dma((nseq,)),
            pltpu.VMEM((rows, 256), BF16), pltpu.VMEM((rows, 256), BF16),
            pltpu.VMEM((256, nq), BF16), pltpu.VMEM((256, nq), BF16), pltpu.VMEM((nq, 128), BF16),
            pltpu.VMEM((cap + span, nq), F32), pltpu.VMEM((cap + span, nq), BF16),
            pltpu.VMEM((128, nq), F32), pltpu.VMEM((nq, 128), F32), pltpu.VMEM((rows, 256), BF16),
        ],
        compiler_params=pltpu.CompilerParams(vmem_limit_bytes=VMEM_LIMIT),
        name="attend",
    )(counts, kvall, q.reshape(nq, 128), grad_out, logit)

    dkv, router = pl.pallas_call(
        functools.partial(return_kernel, nseq, ntp),
        out_shape=(shape((2, cap, 128), BF16), shape((width // 128, 128), F32)),
        in_specs=[anywhere, anywhere, vmem(), anywhere],
        out_specs=tuple(vmem(2)),
        scratch_shapes=[
            pltpu.VMEM((nchip, cap, 256), BF16), pltpu.VMEM((cap, 256), F32), pltpu.VMEM((cap, width), BF16), dma((3,)),
            pltpu.VMEM((nchip + 1, cap, 256), BF16), pltpu.VMEM((nchip, cap, 256), BF16),
            pltpu.VMEM((side, side, cap, 256), BF16), pltpu.VMEM((side, cap, 256), BF16),
            pltpu.VMEM((side, cap, 256), BF16), pltpu.VMEM((ntp, 8, 256), F32),
            pltpu.VMEM((2, width // 128, 128), F32), pltpu.VMEM((nchip, width // 128, 128), F32), pltpu.VMEM((cap, 256), F32),
            dma((nchip,)), dma((nchip,)), dma((nchip,)), dma((nchip,)), dma((side,)), dma((side,)), dma((ntp,)), dma((ntp,)),
            dma, dma, dma((nchip,)), dma((nchip,)),
        ],
        compiler_params=pltpu.CompilerParams(
            collective_id=1, has_side_effects=True, vmem_limit_bytes=VMEM_LIMIT),
        name="settle",
    )(contrib, own, gterm, x)
    return branch, dq, dkv, router.reshape(width)


def solution(mesh):
    in_specs = (
        P("seq", "tp"),
        P("seq", "tp"),
        P(None, "seq", "tp"),
        P("tp"),
        P("seq", None),
        P(),
        P("seq", "tp"),
    )
    out_specs = (P("seq", "tp"), P("seq", "tp"), P(None, "seq", "tp"), P("tp"))
    return jax.shard_map(shards, mesh=mesh, in_specs=in_specs, out_specs=out_specs, check_vma=False)
```

```python
import functools
import math

import jax
import jax.numpy as jnp
from jax import lax
from jax.experimental import pallas as pl
from jax.experimental.pallas import tpu as pltpu
from jax.sharding import PartitionSpec as P

HEAD_WIDTH = 128
MESH = pl.DeviceIdType.MESH
NEG = -1e30
VMEM_LIMIT = 62 * 2 ** 20
CHUNK = 256
LIVE_SHARE = (5, 8)
F32 = jnp.float32
BF16 = jnp.bfloat16


def dot_nn(a, b):
    return lax.dot_general(a, b, (((1,), (0,)), ((), ())), preferred_element_type=F32)


def dot_nt(a, b):
    return lax.dot_general(a, b, (((1,), (1,)), ((), ())), preferred_element_type=F32)


def dot_tn(a, b):
    return lax.dot_general(a, b, (((0,), (0,)), ((), ())), preferred_element_type=F32)


def rows_of(row, cap):
    return jnp.broadcast_to(row, (128, cap)).T


class Grid:
    def __init__(self, me, nchip):
        self.side = math.isqrt(nchip)
        self.chip, self.core = me // 2, me % 2
        self.sib = me + 1 - 2 * self.core
        high, low = self.chip // self.side, self.chip % self.side
        self.a = jnp.where(self.core == 0, high, low)
        self.b = jnp.where(self.core == 0, low, high)

    def at(self, a, b):
        return jnp.where(self.core == 0, self.side * a + b, self.side * b + a)

    def device(self, chip):
        return {"seq": 2 * chip + self.core}


def fetch_kernel(nseq, ntp, hid, qry, kv, w, routed, x_out, q_out, kvall, logit_out,
                 hid_v, qry_v, kv_v, held, part, lsem, ssem, ssem2, rsem, fsem, gsem, tssem, trsem):
    me, mt = lax.axis_index("seq"), lax.axis_index("tp")
    nchip = nseq // 2
    chip, core = me // 2, me % 2
    sib = me + 1 - 2 * core
    cap = routed.shape[1]
    tok = hid.shape[0]
    heads = q_out.shape[0]
    load_kv = pltpu.make_async_copy(kv, kv_v, lsem.at[0])
    load_hid = pltpu.make_async_copy(hid, hid_v, lsem.at[1])
    load_qry = pltpu.make_async_copy(qry, qry_v, lsem.at[2])
    load_kv.start()
    load_hid.start()
    load_qry.start()

    barrier = pltpu.get_barrier_semaphore()

    grid = Grid(me, nchip)
    side, last = grid.side, grid.side - 1
    for q in range(side):
        @pl.when(q != grid.b)
        def _():
            pl.semaphore_signal(barrier, inc=1, device_id=grid.device(grid.at(grid.a, q)), device_id_type=MESH)

        @pl.when(q != grid.a)
        def _():
            pl.semaphore_signal(barrier, inc=1, device_id=grid.device(grid.at(q, grid.b)), device_id_type=MESH)

    def greet_tp(t, _):
        @pl.when(t != mt)
        def _():
            pl.semaphore_signal(barrier, inc=1, device_id={"tp": t}, device_id_type=MESH)
        return 0

    pl.semaphore_signal(barrier, inc=1, device_id={"seq": sib}, device_id_type=MESH)
    lax.fori_loop(0, ntp, greet_tp, 0)

    col = rows_of(routed[...].astype(F32), cap)
    lane = lax.broadcasted_iota(jnp.int32, (cap, 128), 1).astype(F32)
    onehot = jnp.concatenate(
        [jnp.where(col == lane + 128.0 * j, 1.0, 0.0).astype(BF16) for j in range(tok // 128)], axis=1
    )
    load_kv.wait()
    held[:, 0:128] = dot_nn(onehot, kv_v[0]).astype(BF16)
    held[:, 128:256] = dot_nn(onehot, kv_v[1]).astype(BF16)
    keep = pltpu.make_async_copy(held, kvall.at[me], lsem.at[3])
    keep.start()

    pl.semaphore_wait(barrier, 2 * last + 1 + ntp - 1)

    def to_line(q):
        return pltpu.make_async_remote_copy(
            src_ref=held, dst_ref=kvall.at[me], send_sem=ssem.at[q], recv_sem=rsem.at[chip],
            device_id=grid.device(grid.at(grid.a, q)), device_id_type=MESH)

    def line_used(q):
        return (q != grid.b) & (chip < grid.at(last, q))

    def own_to_sib():
        return pltpu.make_async_remote_copy(
            src_ref=held, dst_ref=kvall.at[me], send_sem=fsem.at[chip], recv_sem=gsem.at[chip],
            device_id={"seq": sib}, device_id_type=MESH)

    def across(p, q):
        c = grid.at(grid.a, q)
        block = kvall.at[2 * c + core]
        return pltpu.make_async_remote_copy(
            src_ref=block, dst_ref=block, send_sem=ssem2.at[p * side + q], recv_sem=rsem.at[c],
            device_id=grid.device(grid.at(p, grid.b)), device_id_type=MESH)

    def own_across(p):
        return pltpu.make_async_remote_copy(
            src_ref=held, dst_ref=kvall.at[me], send_sem=ssem2.at[p * side + grid.b], recv_sem=rsem.at[chip],
            device_id=grid.device(grid.at(p, grid.b)), device_id_type=MESH)

    def across_used(p, q):
        return (p != grid.a) & (grid.at(grid.a, q) < grid.at(p, grid.b))

    for q in range(side):
        @pl.when(line_used(q))
        def _():
            to_line(q).start()

    for p in range(side):
        @pl.when(across_used(p, grid.b))
        def _():
            own_across(p).start()

    @pl.when(core == 0)
    def _():
        own_to_sib().start()

    def landed(c):
        block = kvall.at[2 * c + core]
        return pltpu.make_async_remote_copy(
            src_ref=block, dst_ref=block, send_sem=fsem.at[c], recv_sem=rsem.at[c],
            device_id={"seq": sib}, device_id_type=MESH)

    def forward(c):
        block = kvall.at[2 * c + core]
        return pltpu.make_async_remote_copy(
            src_ref=block, dst_ref=block, send_sem=fsem.at[c], recv_sem=gsem.at[c],
            device_id={"seq": sib}, device_id_type=MESH)

    def forwarded(c):
        block = kvall.at[2 * c + 1 - core]
        return pltpu.make_async_remote_copy(
            src_ref=block, dst_ref=block, send_sem=fsem.at[c], recv_sem=gsem.at[c],
            device_id={"seq": sib}, device_id_type=MESH)

    load_hid.wait()
    x = dot_nn(onehot, hid_v[...]).astype(BF16)
    x_out[...] = x
    logit = dot_nt(jnp.broadcast_to(w[...].reshape(1, w.shape[0]), (16, w.shape[0])), x)
    part[mt, :, :] = jnp.zeros((8, 256), F32)
    part[mt, :, 0:cap] = logit[0:8]

    def to_tp(t):
        return pltpu.make_async_remote_copy(
            src_ref=part.at[mt], dst_ref=part.at[mt], send_sem=tssem.at[t], recv_sem=trsem.at[mt],
            device_id={"tp": t}, device_id_type=MESH)

    def from_tp(t):
        return pltpu.make_async_remote_copy(
            src_ref=part.at[t], dst_ref=part.at[t], send_sem=tssem.at[t], recv_sem=trsem.at[t],
            device_id={"tp": t}, device_id_type=MESH)

    def send_tp(t, _):
        @pl.when(t != mt)
        def _():
            to_tp(t).start()
        return 0

    lax.fori_loop(0, ntp, send_tp, 0)

    for q in range(side):
        c = grid.at(grid.a, q)

        @pl.when((q != grid.b) & (c < grid.at(last, grid.b)))
        def _():
            landed(c).wait_recv()

            for p in range(side):
                @pl.when(across_used(p, q))
                def _():
                    across(p, q).start()

            @pl.when(c < chip)
            def _():
                forward(c).start()

    load_qry.wait()
    for h in range(heads):
        q_out[h] = dot_nn(onehot, qry_v[:, h * 128:(h + 1) * 128]).astype(BF16)

    def wait_tp(t, _):
        @pl.when(t != mt)
        def _():
            from_tp(t).wait_recv()
        return 0

    lax.fori_loop(0, ntp, wait_tp, 0)
    total = part[0]
    for t in range(1, ntp):
        total = total + part[t]
    logit_out[...] = total

    for step in range(1, side):
        for q in range(side):
            c = grid.at(lax.rem(grid.a - step + side, side), q)

            @pl.when(c < chip)
            def _():
                landed(c).wait_recv()
                forward(c).start()

    for q in range(side):
        @pl.when(line_used(q))
        def _():
            to_line(q).wait_send()

    keep.wait()

    @pl.when(core == 0)
    def _():
        own_to_sib().wait_send()

    def finish_tp(t, _):
        @pl.when(t != mt)
        def _():
            to_tp(t).wait_send()
        return 0

    lax.fori_loop(0, ntp, finish_tp, 0)
    for q in range(side):
        for p in range(side):
            @pl.when(across_used(p, q))
            def _():
                across(p, q).wait_send()

    def finish_send(c, _):
        @pl.when(c < chip)
        def _():
            forward(c).wait_send()
        return 0

    def finish(c, _):
        @pl.when(c < chip)
        def _():
            forwarded(c).wait_recv()
        return 0

    lax.fori_loop(0, nchip, finish_send, 0)

    @pl.when(core == 1)
    def _():
        forwarded(chip).wait_recv()

    lax.fori_loop(0, nchip, finish, 0)


def attend_kernel(scale, counts, kv_hbm, q_hbm, g_hbm, logit, branch, dq, contrib_hbm, own, gterm,
                  kvall, q, g, contrib, lsem, csem, kx, vx, qtx, dotx, dob, s_scr, e_scr, ot, wide, dkv):
    me = lax.axis_index("seq")
    cap, width = g.shape
    nq = q.shape[0]
    heads = width // 128
    to_exp2 = scale * math.log2(math.e)
    live_here = counts[me]
    loads = [
        pltpu.make_async_copy(kv_hbm.at[me], kvall.at[me], lsem.at[0]),
        pltpu.make_async_copy(q_hbm, q, lsem.at[1]),
        pltpu.make_async_copy(g_hbm, g, lsem.at[2]),
    ]
    for load in loads:
        load.start()

    def block_load(s):
        return pltpu.make_async_copy(kv_hbm.at[s], kvall.at[s], csem.at[s])

    def start_load(s, _):
        block_load(s).start()
        return 0

    lax.fori_loop(0, me, start_load, 0)

    row = lax.broadcasted_iota(jnp.int32, (cap, 128), 0)
    lane = lax.broadcasted_iota(jnp.int32, (cap, 128), 1)
    ones3 = jnp.where(lane < 3, 1.0, 0.0).astype(BF16)
    loads[0].wait()
    kx[0:cap, 0:128] = kvall[me, :, 0:128]
    kx[0:cap, 128:256] = jnp.zeros((cap, 128), BF16)
    vx[0:cap, 0:128] = kvall[me, :, 128:256]
    vx[0:cap, 128:256] = ones3

    def place(s, off):
        block_load(s).wait()
        off = pl.multiple_of(off, 16)
        n = counts[s]
        kx[pl.ds(off, cap), 0:128] = kvall[s, :, 0:128]
        kx[pl.ds(off, cap), 128:256] = jnp.where((row >= n) & (lane == 0), NEG, 0.0).astype(BF16)
        vx[pl.ds(off, cap), 0:128] = kvall[s, :, 128:256]
        vx[pl.ds(off, cap), 128:256] = ones3
        return off + ((n + 15) // 16) * 16

    end = pl.multiple_of(lax.fori_loop(0, me, place, cap), 16)
    kx[pl.ds(end, CHUNK), 0:128] = jnp.zeros((CHUNK, 128), BF16)
    kx[pl.ds(end, CHUNK), 128:256] = jnp.where(
        lax.broadcasted_iota(jnp.int32, (CHUNK, 128), 1) == 0, NEG, 0.0).astype(BF16)
    vx[pl.ds(end, CHUNK), :] = jnp.zeros((CHUNK, 256), BF16)
    chunks = (end - cap + CHUNK - 1) // CHUNK
    doubles = chunks // 2

    def at(c, size):
        return pl.ds(pl.multiple_of(cap + c * CHUNK, 32), size * CHUNK)

    def sweep(step, carry):
        quads = chunks // 4
        carry = lax.fori_loop(0, quads, lambda c, held: step(at(4 * c, 4), 4 * CHUNK, held), carry)
        carry = lax.fori_loop(
            2 * quads, doubles, lambda c, held: step(at(2 * c, 2), 2 * CHUNK, held), carry)
        return lax.fori_loop(2 * doubles, chunks, lambda c, held: step(at(c, 1), CHUNK, held), carry)

    loads[1].wait()

    qtx[0:128, :] = q[...].T
    first = lax.broadcasted_iota(jnp.int32, (128, nq), 0)
    qtx[128:256, :] = jnp.where(first == 0, 1.0, 0.0).astype(BF16)

    key_slot = lax.broadcasted_iota(jnp.int32, (cap, nq), 0)
    pos = lax.broadcasted_iota(jnp.int32, (cap, nq), 1)
    query_slot = pos
    for h in range(1, heads):
        query_slot = query_slot - jnp.where(pos >= h * cap, cap, 0)
    s = jnp.where(key_slot <= query_slot, dot_nn(kx[0:cap, :], qtx[...]), NEG)
    s_scr[0:cap, :] = s
    top = jnp.max(s.reshape(cap // 8, 8, nq), axis=0)

    def score(sl, rows, top):
        s = dot_nn(kx[sl, :], qtx[...])
        s_scr[sl, :] = s
        return jnp.maximum(top, jnp.max(s.reshape(rows // 8, 8, nq), axis=0))

    top = sweep(score, top)
    top = jnp.max(top, axis=0, keepdims=True) * to_exp2

    def soften(sl, rows, total, start):
        e = jnp.exp2(s_scr[sl, :] * to_exp2 - top)
        eb = e.astype(BF16)
        e_scr[sl, :] = eb
        add = dot_tn(vx[sl, 0:128], eb)
        ot[...] = add if start else ot[...] + add
        return total + jnp.sum(e.reshape(rows // 8, 8, nq), axis=0)

    total = soften(pl.ds(0, cap), cap, jnp.zeros((8, nq), F32), True)
    total = sweep(lambda sl, rows, t: soften(sl, rows, t, False), total)
    inverse = 1.0 / jnp.sum(total, axis=0, keepdims=True)

    z = logit[0:1, 0:cap]
    gate = 1.0 / (1.0 + jnp.exp(-z))
    live = lax.broadcasted_iota(jnp.int32, (1, cap), 1) < live_here
    weight = rows_of(jnp.where(live, gate, 0.0), cap)
    factor = jnp.where(live, gate * (1.0 - gate), 0.0)
    ot[...] = ot[...] * inverse
    wide[...] = ot[...].T
    loads[2].wait()
    acc = jnp.zeros((cap, 128), F32)
    for h in range(heads):
        rows, lanes = slice(h * cap, (h + 1) * cap), slice(h * 128, (h + 1) * 128)
        o = wide[rows, :]
        up = g[:, lanes].astype(F32)
        branch[:, lanes] = (o * weight).astype(BF16)
        acc = acc + up * o
        wide[rows, :] = up * weight
    gterm[0:8, :] = jnp.zeros((8, 256), F32)
    gterm[0:1, 0:cap] = jnp.sum(acc.T, axis=0, keepdims=True)
    gterm[1:2, 0:cap] = factor
    cot = (wide[...].T * inverse).astype(BF16)
    dotx[0:128, :] = cot
    cotf = cot.astype(F32)
    delta = -jnp.sum(cotf * ot[...], axis=0, keepdims=True)
    d1 = delta.astype(BF16).astype(F32)
    d2 = (delta - d1).astype(BF16).astype(F32)
    d3 = delta - d1 - d2
    dotx[128:256, :] = jnp.where(
        first == 0, d1, jnp.where(first == 1, d2, jnp.where(first == 2, d3, 0.0))).astype(BF16)
    dob[...] = cotf.T.astype(BF16)

    def back(sl, start):
        e = e_scr[sl, :]
        ds = e * dot_nn(vx[sl, :], dotx[...]).astype(BF16)
        add = dot_tn(kx[sl, 0:128], ds)
        wide_t = ot
        wide_t[...] = add if start else wide_t[...] + add
        return dot_nn(ds, q[...]) * scale, dot_nn(e, dob[...])

    dk, dv = back(pl.ds(0, cap), True)
    own[:, 0:128] = dk
    own[:, 128:256] = dv

    def back_chunk(sl, rows, _):
        dk, dv = back(sl, False)
        dkv[sl, 0:128] = dk.astype(BF16)
        dkv[sl, 128:256] = dv.astype(BF16)
        return 0

    sweep(back_chunk, 0)
    row2 = lax.broadcasted_iota(jnp.int32, (cap, 256), 0)

    def block_store(s):
        return pltpu.make_async_copy(contrib.at[s % 2, s // 2], contrib_hbm.at[s % 2, s // 2], csem.at[s])

    def unplace(s, off):
        off = pl.multiple_of(off, 16)
        n = counts[s]
        block = dkv[pl.ds(off, cap), :].astype(F32)
        contrib[s % 2, s // 2] = jnp.where(row2 < n, block, 0.0).astype(BF16)
        block_store(s).start()
        return off + ((n + 15) // 16) * 16

    lax.fori_loop(0, me, unplace, cap)

    wide[...] = (ot[...] * scale).T
    for h in range(heads):
        dq[:, h * 128:(h + 1) * 128] = wide[h * cap:(h + 1) * cap, :].astype(BF16)

    def finish_store(s, _):
        block_store(s).wait()
        return 0

    lax.fori_loop(0, me, finish_store, 0)


def return_kernel(nseq, ntp, contrib, own_hbm, gterm, x_hbm, dkv_out, router_out,
                  half, own, x, lsem, pair, mine, inbox, inbox2, turn, part, gpair, gchip, sums, psem, prsem, ssem, rsem, s2sem, r2sem, tssem, trsem,
                  qsem, qrsem, gssem, grsem):
    me, mt = lax.axis_index("seq"), lax.axis_index("tp")
    nchip = nseq // 2
    chip, core = me // 2, me % 2
    sib = me + 1 - 2 * core
    cap = x.shape[0]
    loads = [
        pltpu.make_async_copy(contrib.at[core], half, lsem.at[0]),
        pltpu.make_async_copy(own_hbm, own, lsem.at[1]),
        pltpu.make_async_copy(x_hbm, x, lsem.at[2]),
    ]
    for load in loads:
        load.start()

    barrier = pltpu.get_barrier_semaphore()

    def greet_chip(c, _):
        @pl.when(c != chip)
        def _():
            pl.semaphore_signal(barrier, inc=1, device_id={"seq": 2 * c + core}, device_id_type=MESH)
        return 0

    def greet_tp(t, _):
        @pl.when(t != mt)
        def _():
            pl.semaphore_signal(barrier, inc=1, device_id={"tp": t}, device_id_type=MESH)
        return 0

    lax.fori_loop(0, nchip, greet_chip, 0)
    pl.semaphore_signal(barrier, inc=1, device_id={"seq": sib}, device_id_type=MESH)
    lax.fori_loop(0, ntp, greet_tp, 0)
    part[mt] = gterm[...]
    pl.semaphore_wait(barrier, nchip - 1 + 1 + ntp - 1)

    def tp_copy(slot, t):
        return pltpu.make_async_remote_copy(
            src_ref=part.at[slot], dst_ref=part.at[slot], send_sem=tssem.at[t], recv_sem=trsem.at[slot],
            device_id={"tp": t}, device_id_type=MESH)

    def send_tp(t, _):
        @pl.when(t != mt)
        def _():
            tp_copy(mt, t).start()
        return 0

    lax.fori_loop(0, ntp, send_tp, 0)

    def pair_copy(c):
        return pltpu.make_async_remote_copy(
            src_ref=contrib.at[1 - core, c], dst_ref=pair.at[c], send_sem=psem.at[c], recv_sem=prsem.at[c],
            device_id={"seq": sib}, device_id_type=MESH)

    def send_pair(c, _):
        @pl.when((c < chip) | ((c == chip) & (core == 1)))
        def _():
            pair_copy(c).start()
        return 0

    lax.fori_loop(0, nchip, send_pair, 0)

    grid = Grid(me, nchip)
    side, last = grid.side, grid.side - 1

    def first_copy(p, q):
        return pltpu.make_async_remote_copy(
            src_ref=mine.at[grid.at(p, q)], dst_ref=inbox.at[grid.a, q], send_sem=ssem.at[p * side + q],
            recv_sem=rsem.at[grid.a * side + q], device_id=grid.device(grid.at(p, grid.b)), device_id_type=MESH)

    def first_landed(p, q):
        return pltpu.make_async_remote_copy(
            src_ref=inbox.at[p, q], dst_ref=inbox.at[p, q], send_sem=ssem.at[p * side + q],
            recv_sem=rsem.at[p * side + q], device_id=grid.device(grid.at(p, grid.b)), device_id_type=MESH)

    def second_copy(q):
        return pltpu.make_async_remote_copy(
            src_ref=turn.at[q], dst_ref=inbox2.at[grid.b], send_sem=s2sem.at[q], recv_sem=r2sem.at[grid.b],
            device_id=grid.device(grid.at(grid.a, q)), device_id_type=MESH)

    def second_landed(q):
        return pltpu.make_async_remote_copy(
            src_ref=inbox2.at[q], dst_ref=inbox2.at[q], send_sem=s2sem.at[q], recv_sem=r2sem.at[q],
            device_id=grid.device(grid.at(grid.a, q)), device_id_type=MESH)

    loads[0].wait()

    def join(c):
        pair_copy(c).wait_recv()
        mine[c] = (half[c].astype(F32) + pair[c].astype(F32)).astype(BF16)

    for p in range(side):
        for q in range(side):
            @pl.when((p != grid.a) & (grid.at(p, q) < chip))
            def _():
                join(grid.at(p, q))
                first_copy(p, q).start()

    for q in range(side):
        @pl.when(grid.at(grid.a, q) < chip)
        def _():
            join(grid.at(grid.a, q))

    def wait_tp(t, _):
        @pl.when(t != mt)
        def _():
            tp_copy(t, t).wait_recv()
        return 0

    lax.fori_loop(0, ntp, wait_tp, 0)
    total = part[0, 0:1, :]
    for t in range(1, ntp):
        total = total + part[t, 0:1, :]
    dlogit = (total * gterm[1:2, :])[:, 0:cap]
    p1 = dlogit.astype(BF16)
    r1 = dlogit - p1.astype(F32)
    p2 = r1.astype(BF16)
    p3 = (r1 - p2.astype(F32)).astype(BF16)
    loads[2].wait()
    xs = x[...]
    share = (dot_nn(jnp.broadcast_to(p1, (16, cap)), xs) + dot_nn(jnp.broadcast_to(p2, (16, cap)), xs)
             + dot_nn(jnp.broadcast_to(p3, (16, cap)), xs))
    for i in range(x.shape[1] // 128):
        gpair[core, i:i + 1, :] = share[0:1, i * 128:(i + 1) * 128]

    def gpair_copy(slot):
        return pltpu.make_async_remote_copy(
            src_ref=gpair.at[slot], dst_ref=gpair.at[slot], send_sem=qsem, recv_sem=qrsem,
            device_id={"seq": sib}, device_id_type=MESH)

    gpair_copy(core).start()

    def finish_pair(c, _):
        @pl.when((c < chip) | ((c == chip) & (core == 1)))
        def _():
            pair_copy(c).wait_send()
        return 0

    lax.fori_loop(0, nchip, finish_pair, 0)

    def finish_tp(t, _):
        @pl.when(t != mt)
        def _():
            tp_copy(mt, t).wait_send()
        return 0

    lax.fori_loop(0, ntp, finish_tp, 0)
    gpair_copy(1 - core).wait_recv()
    gchip[chip] = gpair[0] + gpair[1]

    def gchip_copy(slot, c):
        return pltpu.make_async_remote_copy(
            src_ref=gchip.at[slot], dst_ref=gchip.at[slot], send_sem=gssem.at[c], recv_sem=grsem.at[slot],
            device_id={"seq": 2 * c + core}, device_id_type=MESH)

    def send_gchip(c, _):
        @pl.when(c != chip)
        def _():
            gchip_copy(chip, c).start()
        return 0

    lax.fori_loop(0, nchip, send_gchip, 0)

    for q in range(side):
        target = grid.at(grid.a, q)

        @pl.when((q != grid.b) & (target < grid.at(last, grid.b)))
        def _():
            @pl.when(target < chip)
            def _():
                sums[...] = mine[target].astype(F32)

            @pl.when(target >= chip)
            def _():
                sums[...] = jnp.zeros((cap, 256), F32)

            for p in range(side):
                @pl.when((p != grid.a) & (target < grid.at(p, grid.b)))
                def _():
                    first_landed(p, q).wait_recv()
                    sums[...] = sums[...] + inbox[p, q].astype(F32)
            turn[q] = sums[...].astype(BF16)
            second_copy(q).start()

    for q in range(side):
        for p in range(side):
            @pl.when((p != grid.a) & (grid.at(p, q) < chip))
            def _():
                first_copy(p, q).wait_send()

    def finish_gchip(c, _):
        @pl.when(c != chip)
        def _():
            gchip_copy(chip, c).wait_send()
        return 0

    lax.fori_loop(0, nchip, finish_gchip, 0)

    @pl.when(core == 0)
    def _():
        pair_copy(chip).wait_recv()
        pair[nchip] = pair[chip]

    @pl.when(core == 1)
    def _():
        pair[nchip] = jnp.zeros((cap, 256), BF16)

    loads[1].wait()
    sums[...] = own[...] + pair[nchip].astype(F32)

    for p in range(side):
        @pl.when((p != grid.a) & (chip < grid.at(p, grid.b)))
        def _():
            first_landed(p, grid.b).wait_recv()
            sums[...] = sums[...] + inbox[p, grid.b].astype(F32)

    for q in range(side):
        @pl.when((q != grid.b) & (chip < grid.at(last, q)))
        def _():
            second_landed(q).wait_recv()
            sums[...] = sums[...] + inbox2[q].astype(F32)
    dkv_out[0] = sums[:, 0:128].astype(BF16)
    dkv_out[1] = sums[:, 128:256].astype(BF16)

    def wait_gchip(c, _):
        @pl.when(c != chip)
        def _():
            gchip_copy(c, c).wait_recv()
        return 0

    lax.fori_loop(0, nchip, wait_gchip, 0)
    total = gchip[0]
    for c in range(1, nchip):
        total = total + gchip[c]
    router_out[...] = total

    gpair_copy(core).wait_send()
    for q in range(side):
        @pl.when((q != grid.b) & (grid.at(grid.a, q) < grid.at(last, grid.b)))
        def _():
            second_copy(q).wait_send()


def hand_kernel(dkv, router, dkv_out, router_out):
    dkv_out[...] = dkv[...]
    router_out[...] = router[...]


def vmem(n=1):
    specs = [pl.BlockSpec(memory_space=pltpu.VMEM) for _ in range(n)]
    return specs if n > 1 else specs[0]


def shards(hidden, queries, keys_values, w_router, routed, counts, grad_out):
    nseq, ntp = lax.axis_size("seq"), lax.axis_size("tp")
    nchip = nseq // 2
    side = math.isqrt(nchip)
    cap = routed.shape[1]
    tok, width = queries.shape
    heads = width // HEAD_WIDTH
    nq = heads * cap
    scale = 1.0 / math.sqrt(HEAD_WIDTH)
    dma, shape = pltpu.SemaphoreType.DMA, jax.ShapeDtypeStruct
    anywhere = pl.BlockSpec(memory_space=pl.ANY)

    x, q, kvall, logit = pl.pallas_call(
        functools.partial(fetch_kernel, nseq, ntp),
        out_shape=(shape((cap, width), BF16), shape((heads, cap, 128), BF16),
                   shape((nseq, cap, 256), BF16), shape((8, 256), F32)),
        in_specs=[anywhere] * 3 + vmem(2),
        out_specs=tuple(vmem(2)) + (anywhere, vmem()),
        scratch_shapes=[
            pltpu.VMEM((tok, width), BF16), pltpu.VMEM((tok, width), BF16), pltpu.VMEM((2, tok, 128), BF16),
            pltpu.VMEM((cap, 256), BF16), pltpu.VMEM((ntp, 8, 256), F32), dma((4,)), dma((nchip,)), dma((nchip,)), dma((nchip,)), dma((nchip,)),
            dma((nchip,)), dma((ntp,)), dma((ntp,)),
        ],
        compiler_params=pltpu.CompilerParams(
            collective_id=0, has_side_effects=True, vmem_limit_bytes=VMEM_LIMIT),
        name="fetch",
    )(hidden, queries, keys_values, w_router, routed)

    live = nseq * cap * LIVE_SHARE[0] // LIVE_SHARE[1]
    span = -(-(live + 15 * nseq) // CHUNK) * CHUNK
    rows = cap + span + CHUNK
    branch, dq, contrib, own, gterm = pl.pallas_call(
        functools.partial(attend_kernel, scale),
        out_shape=(shape((cap, width), BF16), shape((cap, width), BF16),
                   shape((2, nchip, cap, 256), BF16), shape((cap, 256), F32), shape((8, 256), F32)),
        in_specs=[pl.BlockSpec(memory_space=pltpu.SMEM)] + [anywhere] * 3 + [vmem()],
        out_specs=tuple(vmem(2)) + (anywhere,) + tuple(vmem(2)),
        scratch_shapes=[
            pltpu.VMEM((nseq, cap, 256), BF16), pltpu.VMEM((nq, 128), BF16), pltpu.VMEM((cap, width), BF16),
            pltpu.VMEM((2, nchip, cap, 256), BF16), dma((3,)), dma((nseq,)),
            pltpu.VMEM((rows, 256), BF16), pltpu.VMEM((rows, 256), BF16),
            pltpu.VMEM((256, nq), BF16), pltpu.VMEM((256, nq), BF16), pltpu.VMEM((nq, 128), BF16),
            pltpu.VMEM((cap + span, nq), F32), pltpu.VMEM((cap + span, nq), BF16),
            pltpu.VMEM((128, nq), F32), pltpu.VMEM((nq, 128), F32), pltpu.VMEM((rows, 256), BF16),
        ],
        compiler_params=pltpu.CompilerParams(vmem_limit_bytes=VMEM_LIMIT),
        name="attend",
    )(counts, kvall, q.reshape(nq, 128), grad_out, logit)

    dkv, router = pl.pallas_call(
        functools.partial(return_kernel, nseq, ntp),
        out_shape=(shape((2, cap, 128), BF16), shape((width // 128, 128), F32)),
        in_specs=[anywhere, anywhere, vmem(), anywhere],
        out_specs=tuple(vmem(2)),
        scratch_shapes=[
            pltpu.VMEM((nchip, cap, 256), BF16), pltpu.VMEM((cap, 256), F32), pltpu.VMEM((cap, width), BF16), dma((3,)),
            pltpu.VMEM((nchip + 1, cap, 256), BF16), pltpu.VMEM((nchip, cap, 256), BF16),
            pltpu.VMEM((side, side, cap, 256), BF16), pltpu.VMEM((side, cap, 256), BF16),
            pltpu.VMEM((side, cap, 256), BF16), pltpu.VMEM((ntp, 8, 256), F32),
            pltpu.VMEM((2, width // 128, 128), F32), pltpu.VMEM((nchip, width // 128, 128), F32), pltpu.VMEM((cap, 256), F32),
            dma((nchip,)), dma((nchip,)), dma((nchip,)), dma((nchip,)), dma((side,)), dma((side,)), dma((ntp,)), dma((ntp,)),
            dma, dma, dma((nchip,)), dma((nchip,)),
        ],
        compiler_params=pltpu.CompilerParams(
            collective_id=1, has_side_effects=True, vmem_limit_bytes=VMEM_LIMIT),
        name="settle",
    )(contrib, own, gterm, x)
    dkv, router = pl.pallas_call(
        hand_kernel,
        out_shape=(shape((2, cap, 128), BF16), shape((width // 128, 128), F32)),
        in_specs=vmem(2),
        out_specs=tuple(vmem(2)),
        name="hand",
    )(dkv, router)
    return branch, dq, dkv, router.reshape(width)


def solution(mesh):
    in_specs = (
        P("seq", "tp"),
        P("seq", "tp"),
        P(None, "seq", "tp"),
        P("tp"),
        P("seq", None),
        P(),
        P("seq", "tp"),
    )
    out_specs = (P("seq", "tp"), P("seq", "tp"), P(None, "seq", "tp"), P("tp"))
    return jax.shard_map(shards, mesh=mesh, in_specs=in_specs, out_specs=out_specs, check_vma=False)
```
